256 devices in a mesh: ta: 4 (over x), gy: 8 (over y, core), gx: 8 (over z).
Axes of the slice: x: 4, y: 4, z: 8, core: 2. Of those that a mesh axis runs over, the one named last changes fastest.
Arguments:
- latents: bfloat16 [8, 128, 128, 256], P('ta', 'gy', 'gx'), may hold values from -32 to 32
- gain_one: float32 [256], replicated, may hold values from 0.1 to 1.9
- shift_one: float32 [256], replicated, may hold values from -3 to 3
- weight_one: bfloat16 [3, 3, 3, 256, 256], replicated, may hold values from -0.078125 to 0.078125
- bias_one: float32 [256], replicated, may hold values from -3 to 3
- gain_two: float32 [256], replicated, may hold values from 0.1 to 1.9
- shift_two: float32 [256], replicated, may hold values from -3 to 3
- weight_two: bfloat16 [3, 3, 3, 256, 128], replicated, may hold values from -0.078125 to 0.078125
- weight_skip: bfloat16 [256, 128], replicated, may hold values from -0.375 to 0.375
- bias_two: float32 [128], replicated, may hold values from -3 to 3
Outputs:
- decoded: bfloat16 [8, 256, 256, 128], P('ta', 'gy', 'gx')
The draws below stay inside these ranges and needn't reach their ends.
All inputs are finite; a program needn't handle non-finite values.
Results may differ from the reference program's by a relative error of at most 0.0056.
Values may be sent and summed in bfloat16 or wider, within the bound.
A program may use at most 64 MiB of HBM per device.

```python
import jax
import jax.numpy as jnp
from jax import lax

C1 = 256
C2 = 128
GROUPS = 32
NT = 8
NH = 128
NW = 128


def draw_latents(key, part):
    key = jax.random.fold_in(key, 11)
    key_noise = jax.random.fold_in(key, 0)
    key_rows = jax.random.fold_in(key, 1)
    key_cols = jax.random.fold_in(key, 2)
    key_frames = jax.random.fold_in(key, 4)
    third = jnp.log(3.0)
    frame_pos = jnp.arange(NT, dtype=jnp.float32) / (NT - 1)
    row_pos = jnp.arange(NH, dtype=jnp.float32) / (NH - 1)
    col_pos = jnp.arange(NW, dtype=jnp.float32) / (NW - 1)
    trend = jnp.exp(third * (frame_pos[:, None, None] + 0.5 * (row_pos[None, :, None] + col_pos[None, None, :])) - 1.25 * third)
    frame_factor = jax.random.uniform(key_frames, (NT,), minval=0.35, maxval=1.0)
    row_factor = jnp.exp(jax.random.uniform(key_rows, (NH,), minval=-0.5, maxval=0.5))
    col_factor = jnp.exp(jax.random.uniform(key_cols, (NW,), minval=-0.5, maxval=0.5))
    noise = jnp.clip(jax.random.normal(key_noise, (NT, NH, NW, C1)), -5.0, 5.0)
    envelope = trend * frame_factor[:, None, None] * row_factor[None, :, None] * col_factor[None, None, :]
    field = noise * envelope[..., None]
    return field.astype(jnp.bfloat16)


def scatter_about(own_key, shape, scale, most, kind=jnp.bfloat16):
    entries = scale * jax.random.normal(own_key, shape, jnp.float32)
    return jnp.clip(entries, min=-most, max=most).astype(kind)


def setup_inputs(seed: int = 0) -> dict:
    keys = jax.random.split(jax.random.key(seed), 11)
    return {
        "latents": draw_latents(jax.random.fold_in(keys[10], 71), 0),
        "gain_one": jnp.clip(1.0 + 0.18 * jax.random.normal(keys[1], (C1,), jnp.float32), 0.1, 1.9),
        "shift_one": scatter_about(keys[2], (C1,), 0.5, 3.0, jnp.float32),
        "weight_one": scatter_about(keys[3], (3, 3, 3, C1, C1), (27 * C1) ** -0.5, 0.078125),
        "bias_one": scatter_about(keys[4], (C1,), 0.5, 3.0, jnp.float32),
        "gain_two": jnp.clip(1.0 + 0.18 * jax.random.normal(keys[5], (C1,), jnp.float32), 0.1, 1.9),
        "shift_two": scatter_about(keys[6], (C1,), 0.5, 3.0, jnp.float32),
        "weight_two": scatter_about(keys[7], (3, 3, 3, C1, C2), (27 * C1) ** -0.5, 0.078125),
        "weight_skip": scatter_about(keys[8], (C1, C2), C1 ** -0.5, 0.375),
        "bias_two": scatter_about(keys[9], (C2,), 0.5, 3.0, jnp.float32),
    }


EPS = 1e-06

def frame_sums(values):

    def one(frame):
        wide = frame.astype(jnp.float32)
        return jnp.stack([lax.optimization_barrier(jnp.sum(wide, axis=(0, 1))), lax.optimization_barrier(jnp.sum(wide * wide, axis=(0, 1)))])
    sums = lax.map(one, values)
    return sums.reshape(values.shape[0], 2, GROUPS, -1).sum(-1)

def normalize(values, sums, gain, shift, area):
    frames = values.shape[0]
    width = values.shape[3] // GROUPS
    running = jnp.cumsum(sums, axis=0)
    count = (jnp.arange(frames, dtype=jnp.float32) + 1.0) * (area * width)
    mean = running[:, 0] / count[:, None]
    var = running[:, 1] / count[:, None] - mean * mean
    inv = lax.rsqrt(var + EPS)
    scale = jnp.repeat(inv, width, axis=1) * gain[None, :]
    offset = shift[None, :] - jnp.repeat(mean, width, axis=1) * scale

    def one(args):
        frame, sc, of = args
        return jax.nn.silu(frame.astype(jnp.float32) * sc + of).astype(jnp.bfloat16)
    return lax.map(one, (values, scale, offset))

def causal_conv(normed, kernel):
    padded = jnp.pad(normed, ((2, 0), (1, 1), (1, 1), (0, 0)), mode='edge')
    rows, cols = (normed.shape[1], normed.shape[2])

    def one(index):
        block = lax.dynamic_slice_in_dim(padded, index, 3, 0)
        total = jnp.zeros((rows * cols, kernel.shape[4]), jnp.float32)
        for a in range(3):
            for b in range(3):
                for c in range(3):
                    piece = block[a, b:b + rows, c:c + cols].reshape(rows * cols, -1)
                    total = total + jnp.dot(piece, kernel[a, b, c], preferred_element_type=jnp.float32)
        return total.reshape(rows, cols, -1)
    return lax.map(one, jnp.arange(normed.shape[0], dtype=jnp.int32))

def reference(latents, gain_one, shift_one, weight_one, bias_one, gain_two, shift_two, weight_two, weight_skip, bias_two):
    first = normalize(latents, frame_sums(latents), gain_one, shift_one, NH * NW)
    block_out = (latents.astype(jnp.float32) + causal_conv(first, weight_one) + bias_one).astype(jnp.bfloat16)
    sums_two = 4.0 * frame_sums(block_out)
    upsampled = jnp.repeat(jnp.repeat(block_out, 2, axis=1), 2, axis=2)
    second = normalize(upsampled, sums_two, gain_two, shift_two, 4 * NH * NW)
    conv_part = causal_conv(second, weight_two)
    skip_part = jnp.dot(upsampled.reshape(-1, upsampled.shape[3]), weight_skip, preferred_element_type=jnp.float32)
    decoded = conv_part + skip_part.reshape(conv_part.shape) + bias_two
    return decoded.astype(jnp.bfloat16)
```

```python
import jax
import jax.numpy as jnp
from jax import lax
from jax.experimental import pallas as pl
from jax.experimental.pallas import tpu as pltpu
from jax.sharding import PartitionSpec as P

MESH = pl.DeviceIdType.MESH
F32 = jnp.float32
BF16 = jnp.bfloat16
EPS = 1e-06

NTA, NCHIP, NGX = 4, 4, 8
NGY = 2 * NCHIP
ROWS, COLS, CH, CO = 16, 16, 256, 128
AREA = float(NGY * ROWS * NGX * COLS * (CH // 32))

STEP_A = [(c, k) for k in (4, 3, -3, 2, -2, 1, -1, 0) for c in (1, 0) if (c, k) != (0, 0)]
STEP_B = [(j, k) for j in range(NTA) for k in range(NCHIP) if (j, k) != (0, 0)]
STEP_B_ORDER = sorted(STEP_B, key=lambda p: -(min(p[0], NTA - p[0]) + min(p[1], NCHIP - p[1])))

PIECES = [
    (-1, 0, "row", 1, ROWS + 1),
    (1, 0, "row", ROWS, 0),
    (0, -1, "col", 0, 1),
    (0, 1, "col", 1, 0),
    (-1, -1, "corner", 0, 3),
    (-1, 1, "corner", 1, 2),
    (1, -1, "corner", 2, 1),
    (1, 1, "corner", 3, 0),
]


def wrap(value, size):
    return lax.rem(value + size, size)


def kernel(
    lat, w1h, w2h, wsh, g1h, s1h, b1h, g2h, s2h, b2h, out,
    buf, colp, colr, cb, cr, wide, xs, hal, sums, red, sc, w1, w2, we, ws, prm, b2,
    acc1, acc2, skip, tmp, ob,
    msg, da, db, ssem, rsem, ssem_a, rsem_a, ssem_b, rsem_b, lsem, osem,
):
    t = lax.axis_index("ta")
    gy = lax.axis_index("gy")
    gx = lax.axis_index("gx")
    chip, core = gy // 2, lax.rem(gy, 2)

    def at(dt, dy, dx):
        return (wrap(t + dt, NTA), wrap(gy + dy, NGY), wrap(gx + dx, NGX))

    def on_line(c, k):
        return (t, chip * 2 + (1 - core if c else core), wrap(gx + k, NGX))

    def on_plane(j, k):
        return (wrap(t + j, NTA), wrap(chip + k, NCHIP) * 2 + core, gx)

    ready = pltpu.get_barrier_semaphore()
    senders = [on_line(c, k) for c, k in STEP_A] + [on_plane(j, k) for j, k in STEP_B]
    senders += [at(0, dy, dx) for dy, dx, _, _, _ in PIECES]
    senders += [at(-1, 0, 0)] + [at(-1, dy, dx) for dy, dx, _, _, _ in PIECES]
    load_lat = pltpu.make_async_copy(lat, buf.at[0, 2:4, 1 : ROWS + 1], lsem.at[0])
    load_lat.start()
    for device in senders:
        pl.semaphore_signal(ready, inc=1, device_id=device, device_id_type=MESH)
    loads = [
        pltpu.make_async_copy(src, dst, lsem.at[i + 1])
        for i, (src, dst) in enumerate(
            [(w2h, w2), (wsh, ws), (g1h, prm.at[0]), (s1h, prm.at[1]), (b1h, prm.at[2]),
             (g2h, prm.at[3]), (s2h, prm.at[4]), (b2h, b2), (w1h, w1)]
        )
    ]
    for load in loads:
        load.start()

    lane = lax.broadcasted_iota(jnp.int32, (8, 128), 1)
    pick = lax.rem(lane, 8) == lax.broadcasted_iota(jnp.int32, (8, 128), 0)
    row_id = lax.broadcasted_iota(jnp.int32, (COLS, 128), 0)

    def group_sum(v):
        for d in (1, 2, 4):
            v = v + jnp.where((lane & d) != 0, pltpu.roll(v, d, 1), pltpu.roll(v, 128 - d, 1))
        return v

    def compact(v):
        return jnp.sum(jnp.where(pick, group_sum(v), 0.0), axis=0, keepdims=True)

    def expand(row):
        return group_sum(jnp.where(pick, jnp.broadcast_to(row, (8, 128)), 0.0))

    def take_in(stage, block):
        for f in range(2):

            def step(r, carry):
                s, q = carry
                v = block(f, r)
                place = pl.ds(pl.multiple_of((f * ROWS + r) * COLS, COLS), COLS)
                for h in range(2):
                    wide[h, place] = v[:, h * 128 : h * 128 + 128]
                return s + v, q + v * v

            zero = jnp.zeros((COLS, CH), F32)
            s, q = lax.fori_loop(0, ROWS, step, (zero, zero), unroll=4)
            s = jnp.sum(s, axis=0, keepdims=True)
            q = jnp.sum(q, axis=0, keepdims=True)
            for h in range(2):
                lanes = slice(h * 128, h * 128 + 128)
                sums[f * 2 + h : f * 2 + h + 1] = s[:, lanes]
                sums[4 + f * 2 + h : 5 + f * 2 + h] = q[:, lanes]

    def edges(stage):
        for f in range(2):
            base = f * ROWS * COLS
            for side, c in ((0, 0), (1, COLS - 1)):
                for h in range(2):
                    col = wide.at[h][pl.ds(base + c, ROWS, stride=COLS), :]
                    colp[stage, side, f * ROWS : (f + 1) * ROWS, h * 128 : h * 128 + 128] = col.astype(BF16)
            for k, (r, c) in enumerate(((0, 0), (0, COLS - 1), (ROWS - 1, 0), (ROWS - 1, COLS - 1))):
                p = base + r * COLS + c
                for h in range(2):
                    cb[stage, k, f : f + 1, h * 128 : h * 128 + 128] = wide[h, p : p + 1]

    sends = []

    def send_halo(stage):
        def send(src, dst, device):
            i = len(copies)
            copy = pltpu.make_async_remote_copy(
                src, dst, ssem.at[stage, i], rsem.at[stage, i], device_id=device, device_id_type=MESH
            )
            copy.start()
            copies.append(copy)

        copies = []
        for g, dt in ((1, 0), (0, 1)):
            for dy, dx, kind, a, b in PIECES:
                device = at(dt, dy, dx)
                if kind == "row":
                    send(buf.at[stage, 2:4, a], buf.at[stage, 2 * g : 2 * g + 2, b], device)
                elif kind == "col":
                    send(colp.at[stage, a], colr.at[stage, g, b], device)
                else:
                    send(cb.at[stage, a], cr.at[stage, g, b], device)
        for f in (1, 0):
            send(
                buf.at[stage, 2 + f, 1 : ROWS + 1], buf.at[stage, f, 1 : ROWS + 1], at(1, 0, 0)
            )
        sends.extend(copies)
        return copies

    def start_a(stage):
        msg[stage, 0] = compact(sums[...])
        for i, (c, k) in enumerate(STEP_A):
            pltpu.make_async_remote_copy(
                msg.at[stage, 0], da.at[stage, i], ssem_a.at[stage], rsem_a.at[stage],
                device_id=on_line(c, k), device_id_type=MESH,
            ).start()

    def end_a_start_b(stage):
        n = len(STEP_A)
        everything = da.at[stage]
        pltpu.make_async_copy(everything, everything, rsem_a.at[stage]).wait()
        total = msg[stage, 0]
        for i in range(n):
            total = total + da[stage, i]
        msg[stage, 1] = total
        for j, k in STEP_B_ORDER:
            pltpu.make_async_remote_copy(
                msg.at[stage, 1], db.at[stage, j * NCHIP + k - 1], ssem_b.at[stage], rsem_b.at[stage],
                device_id=on_plane(j, k), device_id_type=MESH,
            ).start()

    def end_b(stage, gain, shift):
        everything = db.at[stage]
        pltpu.make_async_copy(everything, everything, rsem_b.at[stage]).wait()
        planes = []
        for j in range(NTA):
            total = msg[stage, 1] if j == 0 else db[stage, j * NCHIP - 1]
            for k in range(1, NCHIP):
                total = total + db[stage, j * NCHIP + k - 1]
            planes.append(total if j == 0 else jnp.where(t >= j, total, 0.0))
        red[0] = expand(planes[0])
        red[1] = expand(planes[1])
        red[2] = expand(planes[2] + planes[3])
        running = []
        for s in (0, 4):
            before = red[2, s : s + 2] + red[2, s + 2 : s + 4]
            row = []
            for i in (1, 0):
                for f in range(2):
                    before = before + red[i, s + 2 * f : s + 2 * f + 2]
                    row.append(before)
            running.append(row)
        for f in range(4):
            count = jnp.maximum((2 * t + f - 1).astype(F32), 1.0) * AREA
            mean = running[0][f] / count
            var = running[1][f] / count - mean * mean
            scale = lax.rsqrt(var + EPS) * gain
            sc[0, 2 * f : 2 * f + 2] = scale
            sc[1, 2 * f : 2 * f + 2] = shift - mean * scale

    def silu(a):
        return 0.5 * a * (1.0 + jnp.tanh(0.5 * a))

    def normed(v, f, lanes, h):
        return silu(v * sc[0, f * 2 + h : f * 2 + h + 1] + sc[1, f * 2 + h : f * 2 + h + 1])

    def normalize(stage):
        for g in range(2):
            for f in range(2):
                for h in range(2):
                    lanes = slice(h * 128, h * 128 + 128)
                    for side in range(2):
                        base = ((2 * g + f) * 2 + side) * 32
                        v = colr[stage, g, side, f * ROWS : (f + 1) * ROWS, lanes].astype(F32)
                        hal[h, base + 8 : base + 8 + ROWS] = normed(v, 2 * g + f, lanes, h)
                        for place, k in ((7, side), (8 + ROWS, 2 + side)):
                            v = cr[stage, g, k, f : f + 1, lanes]
                            hal[h, base + place : base + place + 1] = normed(v, 2 * g + f, lanes, h)
        for f in range(4):
            fe = jnp.where(t == 0, 2, f) if f < 2 else f
            rows = [[sc[i, pl.ds(fe * 2 + h, 1)] for h in range(2)] for i in range(2)]

            def step(r, carry):
                re = jnp.where((r == 0) & (gy == 0), 1, r)
                re = jnp.where((r == ROWS + 1) & (gy == NGY - 1), ROWS, re)
                for h in range(2):
                    lanes = slice(h * 128, h * 128 + 128)
                    v = buf[stage, fe, re, :, lanes].astype(F32)
                    n = silu(v * rows[0][h] + rows[1][h])
                    left = hal[h, pl.ds(fe * 64 + 7 + re, 1)]
                    right = hal[h, pl.ds(fe * 64 + 39 + re, 1)]
                    left = jnp.where(gx == 0, n[0:1], left)
                    right = jnp.where(gx == NGX - 1, n[COLS - 1 : COLS], right)
                    xs[1, f, r, :, lanes] = n.astype(BF16)
                    xs[0, f, r, :, lanes] = jnp.where(row_id == 0, left, pltpu.roll(n, 1, 0)).astype(BF16)
                    xs[2, f, r, :, lanes] = jnp.where(
                        row_id == COLS - 1, right, pltpu.roll(n, COLS - 1, 0)
                    ).astype(BF16)
                return carry

            lax.fori_loop(0, ROWS + 2, step, 0, unroll=6)

    def fold_weights():
        def step(u, carry):
            a = u // 4
            p = lax.rem(u // 2, 2)
            d = lax.rem(u, 2)
            both = jnp.where(p != d, 1.0, 0.0).astype(F32)
            main = a * 9 + jnp.where(d == 0, 0, 6)
            zero = jnp.zeros((32, 128), BF16)
            for s in range(0, CH, 32):
                k = [
                    w2[main + c, s : s + 32].astype(F32) + both * w2[a * 9 + 3 + c, s : s + 32].astype(F32)
                    for c in range(3)
                ]
                we[u, 0, s : s + 32, 0:128] = k[0].astype(BF16)
                we[u, 0, s : s + 32, 128:256] = zero
                we[u, 1, s : s + 32, 0:128] = (k[1] + k[2]).astype(BF16)
                we[u, 1, s : s + 32, 128:256] = (k[0] + k[1]).astype(BF16)
                we[u, 2, s : s + 32, 0:128] = zero
                we[u, 2, s : s + 32, 128:256] = k[2].astype(BF16)
            return carry

        lax.fori_loop(0, 12, step, 0)

    load_lat.wait()
    take_in(0, lambda f, r: buf[0, 2 + f, 1 + r].astype(F32))
    pl.semaphore_wait(ready, len(senders))
    start_a(0)
    edges(0)
    halo = send_halo(0)
    for load in loads:
        load.wait()
    fold_weights()
    end_a_start_b(0)
    end_b(0, prm[0], prm[1])
    for copy in halo:
        copy.wait_recv()
    normalize(0)
    total = jnp.zeros((2 * ROWS * COLS, CH), F32)
    for a in range(3):
        for b in range(3):
            for c in range(3):
                piece = xs[c, a : a + 2, b : b + ROWS].reshape(2 * ROWS * COLS, CH)
                total = total + jnp.dot(piece, w1[a * 9 + b * 3 + c], preferred_element_type=F32)
    acc1[...] = total

    bias = jnp.concatenate([prm[2, 0:1], prm[2, 1:2]], axis=1)

    def block_out(f, r):
        conv = acc1[pl.ds(pl.multiple_of((f * ROWS + r) * COLS, COLS), COLS)]
        v = (buf[0, 2 + f, 1 + r].astype(F32) + conv + bias).astype(BF16)
        buf[1, 2 + f, 1 + r] = v
        return v.astype(F32)

    take_in(1, block_out)
    start_a(1)
    edges(1)
    halo = send_halo(1)
    end_a_start_b(1)
    skip[...] = (
        jnp.dot(
            buf[1, 2:4, 1 : ROWS + 1].reshape(2 * ROWS * COLS, CH), ws[...], preferred_element_type=F32
        )
        + b2[...]
    )
    end_b(1, prm[3], prm[4])
    for copy in halo:
        copy.wait_recv()
    normalize(1)
    acc2[...] = jnp.zeros_like(acc2)

    def taps(u, carry):
        a = u // 2
        p = lax.rem(u, 2)
        total = acc2[p]
        for d in range(2):
            for c in range(3):
                piece = xs[c, pl.ds(a, 2), pl.ds(p + d, ROWS)].reshape(2 * ROWS * COLS, CH)
                total = total + jnp.dot(piece, we[u * 2 + d, c], preferred_element_type=F32)
        acc2[p] = total
        return carry

    lax.fori_loop(0, 6, taps, 0)

    def finish(u, carry):
        f = u // ROWS
        i = lax.rem(u, ROWS)
        place = pl.ds(pl.multiple_of(u * COLS, COLS), COLS)
        extra = skip[place]
        for p in range(2):
            for q in range(2):
                v = acc2[p, place, q * CO : (q + 1) * CO] + extra
                tmp[lax.rem(u, 2) * 2 + p, pl.ds(q, COLS, stride=2), :] = v
            ob[f, i * 2 + p] = tmp[lax.rem(u, 2) * 2 + p].astype(BF16)
        return carry

    for f in range(2):
        lax.fori_loop(f * ROWS, (f + 1) * ROWS, finish, 0, unroll=4)
        pltpu.make_async_copy(ob.at[f], out.at[f], osem.at[f]).start()

    for copy in sends:
        copy.wait_send()
    for stage in range(2):
        pltpu.make_async_copy(da.at[stage], da.at[stage], ssem_a.at[stage]).wait()
        pltpu.make_async_copy(db.at[stage], db.at[stage], ssem_b.at[stage]).wait()
    for f in range(2):
        pltpu.make_async_copy(ob.at[f], out.at[f], osem.at[f]).wait()


def on_device(
    latents, gain_one, shift_one, weight_one, bias_one, gain_two, shift_two, weight_two, weight_skip, bias_two
):
    vmem = pltpu.VMEM
    dma = pltpu.SemaphoreType.DMA
    n_halo = 2 * len(PIECES) + 2
    halves = lambda v: v.reshape(2, 128)
    return pl.pallas_call(
        kernel,
        out_shape=jax.ShapeDtypeStruct((2, 2 * ROWS, 2 * COLS, CO), BF16),
        in_specs=[pl.BlockSpec(memory_space=pl.ANY)] * 10,
        out_specs=pl.BlockSpec(memory_space=pl.ANY),
        scratch_shapes=[
            vmem((2, 4, ROWS + 2, COLS, CH), BF16),
            vmem((2, 2, 2 * ROWS, CH), BF16),
            vmem((2, 2, 2, 2 * ROWS, CH), BF16),
            vmem((2, 4, 2, CH), F32),
            vmem((2, 2, 4, 2, CH), F32),
            vmem((2, 2 * ROWS * COLS, 128), F32),
            vmem((3, 4, ROWS + 2, COLS, CH), BF16),
            vmem((2, 8 * 32, 128), F32),
            vmem((8, 128), F32),
            vmem((3, 8, 128), F32),
            vmem((2, 8, 128), F32),
            vmem((27, CH, CH), BF16),
            vmem((27, CH, CO), BF16),
            vmem((12, 3, CH, 2 * CO), BF16),
            vmem((CH, CO), BF16),
            vmem((5, 2, 128), F32),
            vmem((1, CO), F32),
            vmem((2 * ROWS * COLS, CH), F32),
            vmem((2, 2 * ROWS * COLS, 2 * CO), F32),
            vmem((2 * ROWS * COLS, CO), F32),
            vmem((4, 2 * COLS, CO), F32),
            vmem((2, 2 * ROWS, 2 * COLS, CO), BF16),
            vmem((2, 2, 1, 128), F32),
            vmem((2, len(STEP_A), 1, 128), F32),
            vmem((2, len(STEP_B), 1, 128), F32),
            dma((2, n_halo)),
            dma((2, n_halo)),
            dma((2,)),
            dma((2,)),
            dma((2,)),
            dma((2,)),
            dma((10,)),
            dma((2,)),
        ],
        compiler_params=pltpu.CompilerParams(
            collective_id=0, has_side_effects=True, vmem_limit_bytes=52 << 20
        ),
    )(
        latents,
        weight_one.reshape(27, CH, CH),
        weight_two.reshape(27, CH, CO),
        weight_skip,
        halves(gain_one),
        halves(shift_one),
        halves(bias_one),
        halves(gain_two),
        halves(shift_two),
        bias_two.reshape(1, CO),
    )


def solution(mesh):
    in_specs = (P("ta", "gy", "gx", None),) + (P(),) * 9
    return jax.shard_map(
        on_device, mesh=mesh, in_specs=in_specs, out_specs=P("ta", "gy", "gx", None), check_vma=False
    )
```

```python
import jax
import jax.numpy as jnp
from jax import lax
from jax.experimental import pallas as pl
from jax.experimental.pallas import tpu as pltpu
from jax.sharding import PartitionSpec as P

MESH = pl.DeviceIdType.MESH
F32 = jnp.float32
BF16 = jnp.bfloat16
EPS = 1e-06

NTA, NCHIP, NGX = 4, 4, 8
NGY = 2 * NCHIP
ROWS, COLS, CH, CO = 16, 16, 256, 128
AREA = float(NGY * ROWS * NGX * COLS * (CH // 32))

PLANE = [(j, k) for j in range(NTA) for k in range(NCHIP) if (j, k) != (0, 0)]
PLANE_FAR_FIRST = sorted(PLANE, key=lambda p: -(min(p[0], NTA - p[0]) + min(p[1], NCHIP - p[1])))
LINE = [(c, k) for k in (4, 3, -3, 2, -2, 1, -1, 0) for c in (1, 0) if (c, k) != (0, 0)]

PIECES = [
    (-1, 0, "row", 1, ROWS + 1),
    (1, 0, "row", ROWS, 0),
    (0, -1, "col", 0, 1),
    (0, 1, "col", 1, 0),
    (-1, -1, "corner", 0, 3),
    (-1, 1, "corner", 1, 2),
    (1, -1, "corner", 2, 1),
    (1, 1, "corner", 3, 0),
]


def wrap(value, size):
    return lax.rem(value + size, size)


def kernel(
    lat, w1h, w2h, wsh, g1h, s1h, b1h, g2h, s2h, b2h, out,
    buf, colp, colr, cb, cr, wide, xs, hal, sums, red, sc, w1, w2, wc, we, wg, ws, prm, b2,
    acc1, acc2, acce, accg, skip, tmp, ob,
    msg, msg3, da, db, ssem, rsem, ssem_a, rsem_a, ssem_b, rsem_b, lsem, osem,
):
    t = lax.axis_index("ta")
    gy = lax.axis_index("gy")
    gx = lax.axis_index("gx")
    chip, core = gy // 2, lax.rem(gy, 2)

    def at(dt, dy, dx):
        return (wrap(t + dt, NTA), wrap(gy + dy, NGY), wrap(gx + dx, NGX))

    def on_line(c, k):
        return (t, chip * 2 + (1 - core if c else core), wrap(gx + k, NGX))

    def on_plane(j, k):
        return (wrap(t + j, NTA), wrap(chip + k, NCHIP) * 2 + core, gx)

    ready = pltpu.get_barrier_semaphore()
    senders = [on_plane(j, k) for j, k in PLANE_FAR_FIRST] + [on_line(c, k) for c, k in LINE]
    senders += [at(0, dy, dx) for dy, dx, _, _, _ in PIECES]
    senders += [at(-1, 0, 0)] + [at(-1, dy, dx) for dy, dx, _, _, _ in PIECES]
    load_lat = pltpu.make_async_copy(lat, buf.at[0, 2:4, 1 : ROWS + 1], lsem.at[0])
    load_lat.start()
    for device in senders:
        pl.semaphore_signal(ready, inc=1, device_id=device, device_id_type=MESH)
    loads = [
        pltpu.make_async_copy(src, dst, lsem.at[i + 1])
        for i, (src, dst) in enumerate(
            [(w2h, w2), (wsh, ws), (g1h, prm.at[0]), (s1h, prm.at[1]), (b1h, prm.at[2]),
             (g2h, prm.at[3]), (s2h, prm.at[4]), (b2h, b2), (w1h, w1)]
        )
    ]
    for load in loads:
        load.start()

    lane = lax.broadcasted_iota(jnp.int32, (8, 128), 1)
    pick = lax.rem(lane, 8) == lax.broadcasted_iota(jnp.int32, (8, 128), 0)
    row_id = lax.broadcasted_iota(jnp.int32, (COLS, 128), 0)

    def group_sum(v):
        for d in (1, 2, 4):
            v = v + jnp.where((lane & d) != 0, pltpu.roll(v, d, 1), pltpu.roll(v, 128 - d, 1))
        return v

    def compact(v):
        return jnp.sum(jnp.where(pick, group_sum(v), 0.0), axis=0, keepdims=True)

    def expand(row):
        return group_sum(jnp.where(pick, jnp.broadcast_to(row, (8, 128)), 0.0))

    def take_in(stage, block):
        for f in range(2):

            def step(r, carry):
                s, q = carry
                v = block(f, r)
                place = pl.ds(pl.multiple_of((f * ROWS + r) * COLS, COLS), COLS)
                for h in range(2):
                    wide[h, place] = v[:, h * 128 : h * 128 + 128]
                return s + v, q + v * v

            zero = jnp.zeros((COLS, CH), F32)
            s, q = lax.fori_loop(0, ROWS, step, (zero, zero), unroll=4)
            s = jnp.sum(s, axis=0, keepdims=True)
            q = jnp.sum(q, axis=0, keepdims=True)
            for h in range(2):
                lanes = slice(h * 128, h * 128 + 128)
                sums[f * 2 + h : f * 2 + h + 1] = s[:, lanes]
                sums[4 + f * 2 + h : 5 + f * 2 + h] = q[:, lanes]

    def edges(stage):
        for f in range(2):
            base = f * ROWS * COLS
            for side, c in ((0, 0), (1, COLS - 1)):
                for h in range(2):
                    col = wide.at[h][pl.ds(base + c, ROWS, stride=COLS), :]
                    colp[stage, side, f * ROWS : (f + 1) * ROWS, h * 128 : h * 128 + 128] = col.astype(BF16)
            for k, (r, c) in enumerate(((0, 0), (0, COLS - 1), (ROWS - 1, 0), (ROWS - 1, COLS - 1))):
                p = base + r * COLS + c
                for h in range(2):
                    cb[stage, k, f : f + 1, h * 128 : h * 128 + 128] = wide[h, p : p + 1]

    sends = []

    def send_halo(stage):
        def send(src, dst, device):
            i = len(copies)
            copy = pltpu.make_async_remote_copy(
                src, dst, ssem.at[stage, i], rsem.at[stage, i], device_id=device, device_id_type=MESH
            )
            copy.start()
            copies.append(copy)

        copies = []
        for g, dt in ((1, 0), (0, 1)):
            for dy, dx, kind, a, b in PIECES:
                device = at(dt, dy, dx)
                if kind == "row":
                    send(buf.at[stage, 2:4, a], buf.at[stage, 2 * g : 2 * g + 2, b], device)
                elif kind == "col":
                    send(colp.at[stage, a], colr.at[stage, g, b], device)
                else:
                    send(cb.at[stage, a], cr.at[stage, g, b], device)
            if g == 1:
                for f in (1, 0):
                    send(buf.at[stage, 2 + f, 1 : ROWS + 1], buf.at[stage, f, 1 : ROWS + 1], at(1, 0, 0))
        sends.extend(copies)
        near = len(PIECES)
        return copies[:near], copies[near:]

    def start_plane(stage):
        msg[stage] = compact(sums[...])
        for j, k in PLANE_FAR_FIRST:
            pltpu.make_async_remote_copy(
                msg.at[stage], da.at[stage, j * NCHIP + k - 1], ssem_a.at[stage], rsem_a.at[stage],
                device_id=on_plane(j, k), device_id_type=MESH,
            ).start()

    def start_line(stage):
        everything = da.at[stage]
        pltpu.make_async_copy(everything, everything, rsem_a.at[stage]).wait()
        spans = []
        for j in range(NTA):
            total = msg[stage] if j == 0 else da[stage, j * NCHIP - 1]
            for k in range(1, NCHIP):
                total = total + da[stage, j * NCHIP + k - 1]
            spans.append(total if j == 0 else jnp.where(t >= j, total, 0.0))
        msg3[stage] = jnp.concatenate([spans[0], spans[1], spans[2] + spans[3]], axis=1)
        for i, (c, k) in enumerate(LINE):
            pltpu.make_async_remote_copy(
                msg3.at[stage], db.at[stage, i], ssem_b.at[stage], rsem_b.at[stage],
                device_id=on_line(c, k), device_id_type=MESH,
            ).start()

    def end_line(stage, gain, shift):
        everything = db.at[stage]
        pltpu.make_async_copy(everything, everything, rsem_b.at[stage]).wait()
        total = msg3[stage]
        for i in range(len(LINE)):
            total = total + db[stage, i]
        for i in range(3):
            red[i] = expand(total[:, i * 128 : i * 128 + 128])
        running = []
        for s in (0, 4):
            before = red[2, s : s + 2] + red[2, s + 2 : s + 4]
            row = []
            for i in (1, 0):
                for f in range(2):
                    before = before + red[i, s + 2 * f : s + 2 * f + 2]
                    row.append(before)
            running.append(row)
        for f in range(4):
            count = jnp.maximum((2 * t + f - 1).astype(F32), 1.0) * AREA
            mean = running[0][f] / count
            var = running[1][f] / count - mean * mean
            scale = lax.rsqrt(var + EPS) * gain
            sc[0, 2 * f : 2 * f + 2] = scale
            sc[1, 2 * f : 2 * f + 2] = shift - mean * scale

    def silu(a):
        return 0.5 * a * (1.0 + jnp.tanh(0.5 * a))

    def normalize(stage, g):
        for f in range(2):
            for h in range(2):
                lanes = slice(h * 128, h * 128 + 128)
                frame = 2 * g + f
                scale, shift = sc[0, pl.ds(frame * 2 + h, 1)], sc[1, pl.ds(frame * 2 + h, 1)]
                for side in range(2):
                    base = pl.multiple_of((frame * 2 + side) * 32, 32)
                    v = colr[stage, g, side, f * ROWS : (f + 1) * ROWS, lanes].astype(F32)
                    hal[h, pl.ds(base + 8, ROWS)] = silu(v * scale + shift)
                    for place, k in ((7, side), (8 + ROWS, 2 + side)):
                        v = cr[stage, g, k, f : f + 1, lanes]
                        hal[h, pl.ds(base + place, 1)] = silu(v * scale + shift)

        def frame_step(f, carry):
            frame = 2 * g + f
            fe = jnp.where((t == 0) & (frame < 2), 2, frame)
            rows = [[sc[i, pl.ds(fe * 2 + h, 1)] for h in range(2)] for i in range(2)]

            def step(r, carry):
                re = jnp.where((r == 0) & (gy == 0), 1, r)
                re = jnp.where((r == ROWS + 1) & (gy == NGY - 1), ROWS, re)
                for h in range(2):
                    lanes = slice(h * 128, h * 128 + 128)
                    v = buf[stage, fe, re, :, lanes].astype(F32)
                    n = silu(v * rows[0][h] + rows[1][h])
                    left = hal[h, pl.ds(fe * 64 + 7 + re, 1)]
                    right = hal[h, pl.ds(fe * 64 + 39 + re, 1)]
                    left = jnp.where(gx == 0, n[0:1], left)
                    right = jnp.where(gx == NGX - 1, n[COLS - 1 : COLS], right)
                    xs[1, frame, r, :, lanes] = n.astype(BF16)
                    xs[0, frame, r, :, lanes] = jnp.where(row_id == 0, left, pltpu.roll(n, 1, 0)).astype(BF16)
                    xs[2, frame, r, :, lanes] = jnp.where(
                        row_id == COLS - 1, right, pltpu.roll(n, COLS - 1, 0)
                    ).astype(BF16)
                return carry

            return lax.fori_loop(0, ROWS + 2, step, carry, unroll=6)

        lax.fori_loop(0, 2, frame_step, 0)

    def fold_weights():
        def step(u, carry):
            a = u // 8
            rows = pl.ds(pl.multiple_of(lax.rem(u, 8) * 32, 32), 32)
            k = [[w2[a * 9 + b * 3 + c, rows].astype(F32) for c in range(3)] for b in range(3)]
            upper = [k[1][c] + k[2][c] for c in range(3)]
            lower = [k[0][c] + k[1][c] for c in range(3)]
            for i, v in enumerate((k[0], upper, lower, k[2])):
                wc[a * 4 + i, rows, 0:CO] = (v[1] + v[2]).astype(BF16)
                wc[a * 4 + i, rows, CO : 2 * CO] = (v[0] + v[1]).astype(BF16)
            for q in range(2):
                we[a * 2 + q, rows, 0:CO] = upper[2 * q].astype(BF16)
                we[a * 2 + q, rows, CO : 2 * CO] = lower[2 * q].astype(BF16)
                wg[a * 2 + q, rows, 0:CO] = k[0][2 * q].astype(BF16)
                wg[a * 2 + q, rows, CO : 2 * CO] = k[2][2 * q].astype(BF16)
            return carry

        lax.fori_loop(0, 24, step, 0)

    def dot(x, w):
        return jnp.dot(x, w, preferred_element_type=F32)

    def flat(piece):
        return piece.reshape(-1, CH)

    def conv_one(a):
        total = acc1[...]
        for b in range(3):
            for c in range(3):
                total = total + dot(flat(xs[c, pl.ds(a, 2), b : b + ROWS]), w1[a * 9 + b * 3 + c])
        acc1[...] = total

    def conv_two(a):
        for p in range(2):
            total = acc2[p]
            for d in range(2):
                total = total + dot(flat(xs[1, pl.ds(a, 2), p + d : p + d + ROWS]), wc[a * 4 + p * 2 + d])
            acc2[p] = total
        for q in range(2):
            acce[q] += dot(flat(xs[2 * q, pl.ds(a, 2), 1 : 1 + ROWS]), we[a * 2 + q])
            accg[q] += dot(flat(xs[2 * q, pl.ds(a, 2)]), wg[a * 2 + q])

    def norm_and_convolve(stage, conv, near, far):
        def step(i, carry):
            @pl.when(i == 0)
            def _():
                for copy in near:
                    copy.wait_recv()

            @pl.when(i == 1)
            def _():
                for copy in far:
                    copy.wait_recv()

            @pl.when(i < 2)
            def _():
                normalize(stage, 1 - i)

            conv(2 - i)
            return carry

        lax.fori_loop(0, 3, step, 0)

    load_lat.wait()
    take_in(0, lambda f, r: buf[0, 2 + f, 1 + r].astype(F32))
    pl.semaphore_wait(ready, len(senders))
    start_plane(0)
    edges(0)
    near, far = send_halo(0)
    for load in loads:
        load.wait()
    start_line(0)
    fold_weights()
    acc1[...] = jnp.zeros_like(acc1)
    end_line(0, prm[0], prm[1])
    norm_and_convolve(0, conv_one, near, far)

    bias = jnp.concatenate([prm[2, 0:1], prm[2, 1:2]], axis=1)

    def block_out(f, r):
        conv = acc1[pl.ds(pl.multiple_of((f * ROWS + r) * COLS, COLS), COLS)]
        v = (buf[0, 2 + f, 1 + r].astype(F32) + conv + bias).astype(BF16)
        buf[1, 2 + f, 1 + r] = v
        return v.astype(F32)

    take_in(1, block_out)
    start_plane(1)
    edges(1)
    near, far = send_halo(1)
    skip[...] = dot(buf[1, 2:4, 1 : ROWS + 1].reshape(2 * ROWS * COLS, CH), ws[...]) + b2[...]
    start_line(1)
    acc2[...] = jnp.zeros_like(acc2)
    acce[...] = jnp.zeros_like(acce)
    accg[...] = jnp.zeros_like(accg)
    end_line(1, prm[3], prm[4])
    norm_and_convolve(1, conv_two, near, far)

    def finish(u, carry):
        f = u // ROWS
        i = lax.rem(u, ROWS)
        place = pl.ds(pl.multiple_of(u * COLS, COLS), COLS)
        extra = skip[place]
        for p in range(2):
            for q in range(2):
                outer = pl.ds(pl.multiple_of((u + 2 * f + 2 * p) * COLS, COLS), COLS)
                v = acc2[p, place, q * CO : (q + 1) * CO] + acce[q, place, p * CO : (p + 1) * CO]
                v = v + (accg[q, outer, p * CO : (p + 1) * CO] + extra)
                tmp[lax.rem(u, 2) * 2 + p, pl.ds(q, COLS, stride=2), :] = v
            ob[f, i * 2 + p] = tmp[lax.rem(u, 2) * 2 + p].astype(BF16)
        return carry

    for f in range(2):
        lax.fori_loop(f * ROWS, (f + 1) * ROWS, finish, 0, unroll=4)
        pltpu.make_async_copy(ob.at[f], out.at[f], osem.at[f]).start()

    for copy in sends:
        copy.wait_send()
    for stage in range(2):
        pltpu.make_async_copy(da.at[stage], da.at[stage], ssem_a.at[stage]).wait()
        pltpu.make_async_copy(db.at[stage], db.at[stage], ssem_b.at[stage]).wait()
    for f in range(2):
        pltpu.make_async_copy(ob.at[f], out.at[f], osem.at[f]).wait()


def on_device(
    latents, gain_one, shift_one, weight_one, bias_one, gain_two, shift_two, weight_two, weight_skip, bias_two
):
    vmem = pltpu.VMEM
    dma = pltpu.SemaphoreType.DMA
    n_halo = 2 * len(PIECES) + 2
    halves = lambda v: v.reshape(2, 128)
    return pl.pallas_call(
        kernel,
        out_shape=jax.ShapeDtypeStruct((2, 2 * ROWS, 2 * COLS, CO), BF16),
        in_specs=[pl.BlockSpec(memory_space=pl.ANY)] * 10,
        out_specs=pl.BlockSpec(memory_space=pl.ANY),
        scratch_shapes=[
            vmem((2, 4, ROWS + 2, COLS, CH), BF16),
            vmem((2, 2, 2 * ROWS, CH), BF16),
            vmem((2, 2, 2, 2 * ROWS, CH), BF16),
            vmem((2, 4, 2, CH), F32),
            vmem((2, 2, 4, 2, CH), F32),
            vmem((2, 2 * ROWS * COLS, 128), F32),
            vmem((3, 4, ROWS + 2, COLS, CH), BF16),
            vmem((2, 8 * 32, 128), F32),
            vmem((8, 128), F32),
            vmem((3, 8, 128), F32),
            vmem((2, 8, 128), F32),
            vmem((27, CH, CH), BF16),
            vmem((27, CH, CO), BF16),
            vmem((12, CH, 2 * CO), BF16),
            vmem((6, CH, 2 * CO), BF16),
            vmem((6, CH, 2 * CO), BF16),
            vmem((CH, CO), BF16),
            vmem((5, 2, 128), F32),
            vmem((1, CO), F32),
            vmem((2 * ROWS * COLS, CH), F32),
            vmem((2, 2 * ROWS * COLS, 2 * CO), F32),
            vmem((2, 2 * ROWS * COLS, 2 * CO), F32),
            vmem((2, 2 * (ROWS + 2) * COLS, 2 * CO), F32),
            vmem((2 * ROWS * COLS, CO), F32),
            vmem((4, 2 * COLS, CO), F32),
            vmem((2, 2 * ROWS, 2 * COLS, CO), BF16),
            vmem((2, 1, 128), F32),
            vmem((2, 1, 384), F32),
            vmem((2, len(PLANE), 1, 128), F32),
            vmem((2, len(LINE), 1, 384), F32),
            dma((2, n_halo)),
            dma((2, n_halo)),
            dma((2,)),
            dma((2,)),
            dma((2,)),
            dma((2,)),
            dma((10,)),
            dma((2,)),
        ],
        compiler_params=pltpu.CompilerParams(
            collective_id=0, has_side_effects=True, vmem_limit_bytes=62 << 20
        ),
    )(
        latents,
        weight_one.reshape(27, CH, CH),
        weight_two.reshape(27, CH, CO),
        weight_skip,
        halves(gain_one),
        halves(shift_one),
        halves(bias_one),
        halves(gain_two),
        halves(shift_two),
        bias_two.reshape(1, CO),
    )


def solution(mesh):
    in_specs = (P("ta", "gy", "gx", None),) + (P(),) * 9
    return jax.shard_map(
        on_device, mesh=mesh, in_specs=in_specs, out_specs=P("ta", "gy", "gx", None), check_vma=False
    )
```

```python
import functools

import jax
import jax.numpy as jnp
from jax import lax
from jax.experimental import pallas as pl
from jax.experimental.pallas import tpu as pltpu
from jax.sharding import PartitionSpec as P

MESH = pl.DeviceIdType.MESH
F32 = jnp.float32
BF16 = jnp.bfloat16
EPS = 1e-06

NTA, NCHIP, NGX = 4, 4, 8
NGY = 2 * NCHIP
ROWS, COLS, CH, CO = 16, 16, 256, 128
AREA = float(NGY * ROWS * NGX * COLS * (CH // 32))

PLANE = [(j, k) for j in range(NTA) for k in range(NCHIP) if (j, k) != (0, 0)]
PLANE_FAR_FIRST = sorted(PLANE, key=lambda p: -(min(p[0], NTA - p[0]) + min(p[1], NCHIP - p[1])))
LINE = [(c, k) for k in (4, 3, -3, 2, -2, 1, -1, 0) for c in (1, 0) if (c, k) != (0, 0)]

PIECES = [
    (-1, 0, "row", 1, ROWS + 1),
    (1, 0, "row", ROWS, 0),
    (0, -1, "col", 0, 1),
    (0, 1, "col", 1, 0),
    (-1, -1, "corner", 0, 3),
    (-1, 1, "corner", 1, 2),
    (1, -1, "corner", 2, 1),
    (1, 1, "corner", 3, 0),
]


def wrap(value, size):
    return lax.rem(value + size, size)


def kernel(
    lat, w1h, w2h, wsh, g1h, s1h, b1h, g2h, s2h, b2h, out,
    buf, colp, colr, cb, cr, wide, xs, hal, sums, red, sc, w1, w2, wc, we, wg, ws, prm, b2,
    acc1, acc2, acce, accg, tmp, ob,
    msg, msg3, da, db, ssem, rsem, ssem_a, rsem_a, ssem_b, rsem_b, lsem, osem,
):
    t = lax.axis_index("ta")
    gy = lax.axis_index("gy")
    gx = lax.axis_index("gx")
    chip, core = gy // 2, lax.rem(gy, 2)

    def at(dt, dy, dx):
        return (wrap(t + dt, NTA), wrap(gy + dy, NGY), wrap(gx + dx, NGX))

    def on_line(c, k):
        return (t, chip * 2 + (1 - core if c else core), wrap(gx + k, NGX))

    def on_plane(j, k):
        return (wrap(t + j, NTA), wrap(chip + k, NCHIP) * 2 + core, gx)

    ready = pltpu.get_barrier_semaphore()
    senders = [on_plane(j, k) for j, k in PLANE_FAR_FIRST] + [on_line(c, k) for c, k in LINE]
    senders += [at(0, dy, dx) for dy, dx, _, _, _ in PIECES]
    senders += [at(-1, 0, 0)] + [at(-1, dy, dx) for dy, dx, _, _, _ in PIECES]
    load_lat = pltpu.make_async_copy(lat, buf.at[0, 2:4, 1 : ROWS + 1], lsem.at[0])
    load_lat.start()
    for device in senders:
        pl.semaphore_signal(ready, inc=1, device_id=device, device_id_type=MESH)
    loads = [
        pltpu.make_async_copy(src, dst, lsem.at[i + 1])
        for i, (src, dst) in enumerate(
            [(w2h, w2), (wsh, ws), (g1h, prm.at[0]), (s1h, prm.at[1]), (b1h, prm.at[2]),
             (g2h, prm.at[3]), (s2h, prm.at[4]), (b2h, b2), (w1h, w1)]
        )
    ]
    for load in loads:
        load.start()

    lane = lax.broadcasted_iota(jnp.int32, (8, 128), 1)
    pick = lax.rem(lane, 8) == lax.broadcasted_iota(jnp.int32, (8, 128), 0)
    row_id = lax.broadcasted_iota(jnp.int32, (COLS, 128), 0)

    def group_sum(v):
        for d in (1, 2, 4):
            v = v + jnp.where((lane & d) != 0, pltpu.roll(v, d, 1), pltpu.roll(v, 128 - d, 1))
        return v

    def compact(v):
        return jnp.sum(jnp.where(pick, group_sum(v), 0.0), axis=0, keepdims=True)

    def expand(row):
        return group_sum(jnp.where(pick, jnp.broadcast_to(row, (8, 128)), 0.0))

    def take_in(stage, block):
        for f in range(2):

            def step(r, carry):
                s, q = carry
                v = block(f, r)
                place = pl.ds(pl.multiple_of((f * ROWS + r) * COLS, COLS), COLS)
                for h in range(2):
                    wide[h, place] = v[:, h * 128 : h * 128 + 128]
                return s + v, q + v * v

            zero = jnp.zeros((COLS, CH), F32)
            s, q = lax.fori_loop(0, ROWS, step, (zero, zero), unroll=4)
            s = jnp.sum(s, axis=0, keepdims=True)
            q = jnp.sum(q, axis=0, keepdims=True)
            for h in range(2):
                lanes = slice(h * 128, h * 128 + 128)
                sums[f * 2 + h : f * 2 + h + 1] = s[:, lanes]
                sums[4 + f * 2 + h : 5 + f * 2 + h] = q[:, lanes]

    def edges(stage):
        for f in range(2):
            base = f * ROWS * COLS
            for side, c in ((0, 0), (1, COLS - 1)):
                for h in range(2):
                    col = wide.at[h][pl.ds(base + c, ROWS, stride=COLS), :]
                    colp[stage, side, f * ROWS : (f + 1) * ROWS, h * 128 : h * 128 + 128] = col.astype(BF16)
            for k, (r, c) in enumerate(((0, 0), (0, COLS - 1), (ROWS - 1, 0), (ROWS - 1, COLS - 1))):
                p = base + r * COLS + c
                for h in range(2):
                    cb[stage, k, f : f + 1, h * 128 : h * 128 + 128] = wide[h, p : p + 1]

    sends = []

    def send_halo(stage):
        def send(src, dst, device):
            i = len(copies)
            copy = pltpu.make_async_remote_copy(
                src, dst, ssem.at[stage, i], rsem.at[stage, i], device_id=device, device_id_type=MESH
            )
            copy.start()
            copies.append(copy)

        copies = []
        for g, dt in ((1, 0), (0, 1)):
            for dy, dx, kind, a, b in PIECES:
                device = at(dt, dy, dx)
                if kind == "row":
                    send(buf.at[stage, 2:4, a], buf.at[stage, 2 * g : 2 * g + 2, b], device)
                elif kind == "col":
                    send(colp.at[stage, a], colr.at[stage, g, b], device)
                else:
                    send(cb.at[stage, a], cr.at[stage, g, b], device)
            if g == 1:
                for f in (1, 0):
                    send(buf.at[stage, 2 + f, 1 : ROWS + 1], buf.at[stage, f, 1 : ROWS + 1], at(1, 0, 0))
        sends.extend(copies)
        near = len(PIECES)
        return copies[:near], copies[near:]

    def start_plane(stage):
        msg[stage] = compact(sums[...])
        for j, k in PLANE_FAR_FIRST:
            pltpu.make_async_remote_copy(
                msg.at[stage], da.at[stage, j * NCHIP + k - 1], ssem_a.at[stage], rsem_a.at[stage],
                device_id=on_plane(j, k), device_id_type=MESH,
            ).start()

    def start_line(stage):
        everything = da.at[stage]
        pltpu.make_async_copy(everything, everything, rsem_a.at[stage]).wait()
        spans = []
        for j in range(NTA):
            total = msg[stage] if j == 0 else da[stage, j * NCHIP - 1]
            for k in range(1, NCHIP):
                total = total + da[stage, j * NCHIP + k - 1]
            spans.append(total if j == 0 else jnp.where(t >= j, total, 0.0))
        msg3[stage] = jnp.concatenate([spans[0], spans[1], spans[2] + spans[3]], axis=1)
        for i, (c, k) in enumerate(LINE):
            pltpu.make_async_remote_copy(
                msg3.at[stage], db.at[stage, i], ssem_b.at[stage], rsem_b.at[stage],
                device_id=on_line(c, k), device_id_type=MESH,
            ).start()

    def end_line(stage, gain, shift):
        everything = db.at[stage]
        pltpu.make_async_copy(everything, everything, rsem_b.at[stage]).wait()
        total = msg3[stage]
        for i in range(len(LINE)):
            total = total + db[stage, i]
        for i in range(3):
            red[i] = expand(total[:, i * 128 : i * 128 + 128])
        running = []
        for s in (0, 4):
            before = red[2, s : s + 2] + red[2, s + 2 : s + 4]
            row = []
            for i in (1, 0):
                for f in range(2):
                    before = before + red[i, s + 2 * f : s + 2 * f + 2]
                    row.append(before)
            running.append(row)
        for f in range(4):
            count = jnp.maximum((2 * t + f - 1).astype(F32), 1.0) * AREA
            mean = running[0][f] / count
            var = running[1][f] / count - mean * mean
            scale = lax.rsqrt(var + EPS) * gain
            sc[0, 2 * f : 2 * f + 2] = scale
            sc[1, 2 * f : 2 * f + 2] = shift - mean * scale

    def silu(a):
        return 0.5 * a * (1.0 + jnp.tanh(0.5 * a))

    def norm_edges(stage, g):
        for f in range(2):
            for h in range(2):
                lanes = slice(h * 128, h * 128 + 128)
                frame = 2 * g + f
                scale, shift = sc[0, pl.ds(frame * 2 + h, 1)], sc[1, pl.ds(frame * 2 + h, 1)]
                for side in range(2):
                    base = pl.multiple_of((frame * 2 + side) * 32, 32)
                    v = colr[stage, g, side, f * ROWS : (f + 1) * ROWS, lanes].astype(F32)
                    hal[h, pl.ds(base + 8, ROWS)] = silu(v * scale + shift)
                    for place, k in ((7, side), (8 + ROWS, 2 + side)):
                        v = cr[stage, g, k, f : f + 1, lanes]
                        hal[h, pl.ds(base + place, 1)] = silu(v * scale + shift)

    def norm_rows(stage, frame):
        fe = jnp.where((t == 0) & (frame < 2), 2, frame)
        rows = [[sc[i, pl.ds(fe * 2 + h, 1)] for h in range(2)] for i in range(2)]

        def step(r):
            re = jnp.where((r == 0) & (gy == 0), 1, r)
            re = jnp.where((r == ROWS + 1) & (gy == NGY - 1), ROWS, re)
            for h in range(2):
                lanes = slice(h * 128, h * 128 + 128)
                v = buf[stage, fe, re, :, lanes].astype(F32)
                n = silu(v * rows[0][h] + rows[1][h])
                left = hal[h, pl.ds(fe * 64 + 7 + re, 1)]
                right = hal[h, pl.ds(fe * 64 + 39 + re, 1)]
                left = jnp.where(gx == 0, n[0:1], left)
                right = jnp.where(gx == NGX - 1, n[COLS - 1 : COLS], right)
                xs[1, frame, r, :, lanes] = n.astype(BF16)
                xs[0, frame, r, :, lanes] = jnp.where(row_id == 0, left, pltpu.roll(n, 1, 0)).astype(BF16)
                xs[2, frame, r, :, lanes] = jnp.where(
                    row_id == COLS - 1, right, pltpu.roll(n, COLS - 1, 0)
                ).astype(BF16)

        return step

    def normalize(stage, g):
        norm_edges(stage, g)

        def frame_step(f, carry):
            row_step = norm_rows(stage, 2 * g + f)

            def step(r, carry):
                row_step(r)
                return carry

            return lax.fori_loop(0, ROWS + 2, step, carry, unroll=6)

        lax.fori_loop(0, 2, frame_step, 0)

    def fold_weights():
        def step(u, carry):
            a = u // 8
            rows = pl.ds(pl.multiple_of(lax.rem(u, 8) * 32, 32), 32)
            k = [[w2[a * 9 + b * 3 + c, rows].astype(F32) for c in range(3)] for b in range(3)]
            upper = [k[1][c] + k[2][c] for c in range(3)]
            lower = [k[0][c] + k[1][c] for c in range(3)]
            for i, v in enumerate((k[0], upper, lower, k[2])):
                wc[a * 4 + i, rows, 0:CO] = (v[1] + v[2]).astype(BF16)
                wc[a * 4 + i, rows, CO : 2 * CO] = (v[0] + v[1]).astype(BF16)
            for q in range(2):
                we[a * 2 + q, rows, 0:CO] = upper[2 * q].astype(BF16)
                we[a * 2 + q, rows, CO : 2 * CO] = lower[2 * q].astype(BF16)
                wg[a * 2 + q, rows, 0:CO] = k[0][2 * q].astype(BF16)
                wg[a * 2 + q, rows, CO : 2 * CO] = k[2][2 * q].astype(BF16)
            return carry

        lax.fori_loop(0, 24, step, 0)

    def dot(x, w):
        return jnp.dot(x, w, preferred_element_type=F32)

    def flat(piece):
        return piece.reshape(-1, CH)

    def conv_one_row(b):
        total = acc1[...]
        for c in range(3):
            total = total + dot(flat(xs[c, 2:4, b : b + ROWS]), w1[18 + b * 3 + c])
        acc1[...] = total

    def conv_one(a):
        total = acc1[...]
        for b in range(3):
            for c in range(3):
                total = total + dot(flat(xs[c, pl.ds(a, 2), b : b + ROWS]), w1[a * 9 + b * 3 + c])
        acc1[...] = total

    def conv_two(a):
        for p in range(2):
            total = acc2[p]
            for d in range(2):
                total = total + dot(flat(xs[1, pl.ds(a, 2), p + d : p + d + ROWS]), wc[a * 4 + p * 2 + d])
            acc2[p] = total
        for q in range(2):
            acce[q] += dot(flat(xs[2 * q, pl.ds(a, 2), 1 : 1 + ROWS]), we[a * 2 + q])
            accg[q] += dot(flat(xs[2 * q, pl.ds(a, 2)]), wg[a * 2 + q])

    def beside(products, work):
        done = 0
        for i, product in enumerate(products):
            product()
            until = (i + 1) * len(work) // len(products)
            for n in range(done, until):
                work[n]()
            done = until

    def rows_before(stage):
        work = []
        for f in range(2):
            step = norm_rows(stage, f)
            work += [functools.partial(step, r) for r in range(ROWS + 2)]
        return work

    def products_two(a):
        def middle(p):
            total = acc2[p]
            for d in range(2):
                total = total + dot(flat(xs[1, a : a + 2, p + d : p + d + ROWS]), wc[a * 4 + p * 2 + d])
            acc2[p] = total

        def inner(q):
            acce[q] += dot(flat(xs[2 * q, a : a + 2, 1 : 1 + ROWS]), we[a * 2 + q])

        def outer(q):
            accg[q] += dot(flat(xs[2 * q, a : a + 2]), wg[a * 2 + q])

        return [functools.partial(f, i) for f in (middle, inner, outer) for i in range(2)]

    def chain_two():
        def middle(p, f, frames):
            place = slice(f * ROWS * COLS, (f + frames) * ROWS * COLS)
            total = acc2[p, place]
            for a in (1, 0):
                for d in range(2):
                    piece = xs[1, a + f : a + f + frames, p + d : p + d + ROWS]
                    total = total + dot(flat(piece), wc[a * 4 + p * 2 + d])
            acc2[p, place] = total

        def outputs(p, f):
            return [functools.partial(finish, p, f, i) for i in range(ROWS)]

        for q in range(2):
            total = acce[q]
            for a in (1, 0):
                total = total + dot(flat(xs[2 * q, a : a + 2, 1 : 1 + ROWS]), we[a * 2 + q])
            acce[q] = total
            total = accg[q]
            for a in (1, 0):
                total = total + dot(flat(xs[2 * q, a : a + 2]), wg[a * 2 + q])
            accg[q] = total
        middle(0, 0, 2)
        middle(1, 0, 1)
        for work in outputs(0, 0) + outputs(0, 1):
            work()
        middle(1, 1, 1)
        for work in outputs(1, 0):
            work()
        pltpu.make_async_copy(ob.at[0], out.at[0], osem.at[0]).start()
        for work in outputs(1, 1):
            work()
        pltpu.make_async_copy(ob.at[1], out.at[1], osem.at[1]).start()

    def finish(p, f, i):
        slot = i % 8
        place = slice((f * ROWS + i) * COLS, (f * ROWS + i + 1) * COLS)
        row = f * (ROWS + 2) + i + 2 * p
        outer = slice(row * COLS, (row + 1) * COLS)
        for q in range(2):
            v = acc2[p, place, q * CO : (q + 1) * CO] + acce[q, place, p * CO : (p + 1) * CO]
            tmp[slot, pl.ds(q, COLS, stride=2), :] = v + accg[q, outer, p * CO : (p + 1) * CO]
        ob[f, i * 2 + p] = tmp[slot].astype(BF16)

    load_lat.wait()
    take_in(0, lambda f, r: buf[0, 2 + f, 1 + r].astype(F32))
    pl.semaphore_wait(ready, len(senders))
    start_plane(0)
    edges(0)
    near, far = send_halo(0)
    for load in loads:
        load.wait()
    start_line(0)
    fold_weights()
    acc1[...] = jnp.zeros_like(acc1)
    end_line(0, prm[0], prm[1])
    for copy in near:
        copy.wait_recv()
    normalize(0, 1)
    for copy in far:
        copy.wait_recv()
    norm_edges(0, 0)
    beside([functools.partial(conv_one_row, b) for b in range(3)], rows_before(0))

    def tap_step(i, carry):
        conv_one(1 - i)
        return carry

    lax.fori_loop(0, 2, tap_step, 0)

    bias = jnp.concatenate([prm[2, 0:1], prm[2, 1:2]], axis=1)

    def block_out(f, r):
        conv = acc1[pl.ds(pl.multiple_of((f * ROWS + r) * COLS, COLS), COLS)]
        v = (buf[0, 2 + f, 1 + r].astype(F32) + conv + bias).astype(BF16)
        buf[1, 2 + f, 1 + r] = v
        return v.astype(F32)

    take_in(1, block_out)
    start_plane(1)
    edges(1)
    near, far = send_halo(1)
    start_line(1)
    skip = dot(flat(buf[1, 2:4, 1 : ROWS + 1]), ws[...]) + b2[...]
    for p in range(2):
        for q in range(2):
            acc2[p, :, q * CO : (q + 1) * CO] = skip
    acce[...] = jnp.zeros_like(acce)
    accg[...] = jnp.zeros_like(accg)
    end_line(1, prm[3], prm[4])
    for copy in near:
        copy.wait_recv()
    normalize(1, 1)
    for copy in far:
        copy.wait_recv()
    norm_edges(1, 0)
    beside(products_two(2), rows_before(1))
    chain_two()

    for copy in sends:
        copy.wait_send()
    for stage in range(2):
        pltpu.make_async_copy(da.at[stage], da.at[stage], ssem_a.at[stage]).wait()
        pltpu.make_async_copy(db.at[stage], db.at[stage], ssem_b.at[stage]).wait()
    for f in range(2):
        pltpu.make_async_copy(ob.at[f], out.at[f], osem.at[f]).wait()


def on_device(
    latents, gain_one, shift_one, weight_one, bias_one, gain_two, shift_two, weight_two, weight_skip, bias_two
):
    vmem = pltpu.VMEM
    dma = pltpu.SemaphoreType.DMA
    n_halo = 2 * len(PIECES) + 2
    halves = lambda v: v.reshape(2, 128)
    return pl.pallas_call(
        kernel,
        out_shape=jax.ShapeDtypeStruct((2, 2 * ROWS, 2 * COLS, CO), BF16),
        in_specs=[pl.BlockSpec(memory_space=pl.ANY)] * 10,
        out_specs=pl.BlockSpec(memory_space=pl.ANY),
        scratch_shapes=[
            vmem((2, 4, ROWS + 2, COLS, CH), BF16),
            vmem((2, 2, 2 * ROWS, CH), BF16),
            vmem((2, 2, 2, 2 * ROWS, CH), BF16),
            vmem((2, 4, 2, CH), F32),
            vmem((2, 2, 4, 2, CH), F32),
            vmem((2, 2 * ROWS * COLS, 128), F32),
            vmem((3, 4, ROWS + 2, COLS, CH), BF16),
            vmem((2, 8 * 32, 128), F32),
            vmem((8, 128), F32),
            vmem((3, 8, 128), F32),
            vmem((2, 8, 128), F32),
            vmem((27, CH, CH), BF16),
            vmem((27, CH, CO), BF16),
            vmem((12, CH, 2 * CO), BF16),
            vmem((6, CH, 2 * CO), BF16),
            vmem((6, CH, 2 * CO), BF16),
            vmem((CH, CO), BF16),
            vmem((5, 2, 128), F32),
            vmem((1, CO), F32),
            vmem((2 * ROWS * COLS, CH), F32),
            vmem((2, 2 * ROWS * COLS, 2 * CO), F32),
            vmem((2, 2 * ROWS * COLS, 2 * CO), F32),
            vmem((2, 2 * (ROWS + 2) * COLS, 2 * CO), F32),
            vmem((8, 2 * COLS, CO), F32),
            vmem((2, 2 * ROWS, 2 * COLS, CO), BF16),
            vmem((2, 1, 128), F32),
            vmem((2, 1, 384), F32),
            vmem((2, len(PLANE), 1, 128), F32),
            vmem((2, len(LINE), 1, 384), F32),
            dma((2, n_halo)),
            dma((2, n_halo)),
            dma((2,)),
            dma((2,)),
            dma((2,)),
            dma((2,)),
            dma((10,)),
            dma((2,)),
        ],
        compiler_params=pltpu.CompilerParams(
            collective_id=0, has_side_effects=True, vmem_limit_bytes=62 << 20
        ),
    )(
        latents,
        weight_one.reshape(27, CH, CH),
        weight_two.reshape(27, CH, CO),
        weight_skip,
        halves(gain_one),
        halves(shift_one),
        halves(bias_one),
        halves(gain_two),
        halves(shift_two),
        bias_two.reshape(1, CO),
    )


def solution(mesh):
    in_specs = (P("ta", "gy", "gx", None),) + (P(),) * 9
    return jax.shard_map(
        on_device, mesh=mesh, in_specs=in_specs, out_specs=P("ta", "gy", "gx", None), check_vma=False
    )
```

```python
import functools

import jax
import jax.numpy as jnp
from jax import lax
from jax.experimental import pallas as pl
from jax.experimental.pallas import tpu as pltpu
from jax.sharding import PartitionSpec as P

MESH = pl.DeviceIdType.MESH
F32 = jnp.float32
BF16 = jnp.bfloat16
EPS = 1e-06

NTA, NCHIP, NGX = 4, 4, 8
NGY = 2 * NCHIP
ROWS, COLS, CH, CO = 16, 16, 256, 128
AREA = float(NGY * ROWS * NGX * COLS * (CH // 32))

PLANE = [(j, k) for j in range(NTA) for k in range(NCHIP) if (j, k) != (0, 0)]
PLANE_FAR_FIRST = sorted(PLANE, key=lambda p: -(min(p[0], NTA - p[0]) + min(p[1], NCHIP - p[1])))
LINE = [(c, k) for k in (4, 3, -3, 2, -2, 1, -1, 0) for c in (1, 0) if (c, k) != (0, 0)]

PIECES = [
    (-1, 0, "row", 1, ROWS + 1),
    (1, 0, "row", ROWS, 0),
    (0, -1, "col", 0, 1),
    (0, 1, "col", 1, 0),
    (-1, -1, "corner", 0, 3),
    (-1, 1, "corner", 1, 2),
    (1, -1, "corner", 2, 1),
    (1, 1, "corner", 3, 0),
]


def wrap(value, size):
    return lax.rem(value + size, size)


def kernel(
    lat, w1h, w2h, wsh, g1h, s1h, b1h, g2h, s2h, b2h, out,
    buf, colp, colr, cb, cr, wide, xs, hal, sums, red, sc, w1, w2, wc, we, wg, ws, prm, b2,
    acc1, acc2, acce, accg, tmp, ob,
    msg, msg3, da, db, ssem, rsem, ssem_a, rsem_a, ssem_b, rsem_b, lsem, osem,
):
    t = lax.axis_index("ta")
    gy = lax.axis_index("gy")
    gx = lax.axis_index("gx")
    chip, core = gy // 2, lax.rem(gy, 2)

    def at(dt, dy, dx):
        return (wrap(t + dt, NTA), wrap(gy + dy, NGY), wrap(gx + dx, NGX))

    def on_line(c, k):
        return (t, chip * 2 + (1 - core if c else core), wrap(gx + k, NGX))

    def on_plane(j, k):
        return (wrap(t + j, NTA), wrap(chip + k, NCHIP) * 2 + core, gx)

    ready = pltpu.get_barrier_semaphore()
    senders = [on_plane(j, k) for j, k in PLANE_FAR_FIRST] + [on_line(c, k) for c, k in LINE]
    senders += [at(0, dy, dx) for dy, dx, _, _, _ in PIECES]
    senders += [at(-1, 0, 0)] + [at(-1, dy, dx) for dy, dx, _, _, _ in PIECES]
    load_lat = pltpu.make_async_copy(lat, buf.at[0, 2:4, 1 : ROWS + 1], lsem.at[0])
    load_lat.start()
    for device in senders:
        pl.semaphore_signal(ready, inc=1, device_id=device, device_id_type=MESH)
    loads = [
        pltpu.make_async_copy(src, dst, lsem.at[i + 1])
        for i, (src, dst) in enumerate(
            [(w2h, w2), (wsh, ws), (g1h, prm.at[0]), (s1h, prm.at[1]), (b1h, prm.at[2]),
             (g2h, prm.at[3]), (s2h, prm.at[4]), (b2h, b2), (w1h, w1)]
        )
    ]
    for load in loads:
        load.start()

    lane = lax.broadcasted_iota(jnp.int32, (8, 128), 1)
    pick = lax.rem(lane, 8) == lax.broadcasted_iota(jnp.int32, (8, 128), 0)
    row_id = lax.broadcasted_iota(jnp.int32, (COLS, 128), 0)

    def group_sum(v):
        for d in (1, 2, 4):
            v = v + jnp.where((lane & d) != 0, pltpu.roll(v, d, 1), pltpu.roll(v, 128 - d, 1))
        return v

    def compact(v):
        return jnp.sum(jnp.where(pick, group_sum(v), 0.0), axis=0, keepdims=True)

    def expand(row):
        return group_sum(jnp.where(pick, jnp.broadcast_to(row, (8, 128)), 0.0))

    def take_in(stage, block):
        for f in range(2):

            def step(r, carry):
                s, q = carry
                v = block(f, r)
                place = pl.ds(pl.multiple_of((f * ROWS + r) * COLS, COLS), COLS)
                for h in range(2):
                    wide[h, place] = v[:, h * 128 : h * 128 + 128]
                return s + v, q + v * v

            zero = jnp.zeros((COLS, CH), F32)
            s, q = lax.fori_loop(0, ROWS, step, (zero, zero), unroll=4)
            s = jnp.sum(s, axis=0, keepdims=True)
            q = jnp.sum(q, axis=0, keepdims=True)
            for h in range(2):
                lanes = slice(h * 128, h * 128 + 128)
                sums[f * 2 + h : f * 2 + h + 1] = s[:, lanes]
                sums[4 + f * 2 + h : 5 + f * 2 + h] = q[:, lanes]

    def edges(stage):
        for f in range(2):
            base = f * ROWS * COLS
            for side, c in ((0, 0), (1, COLS - 1)):
                for h in range(2):
                    col = wide.at[h][pl.ds(base + c, ROWS, stride=COLS), :]
                    colp[stage, side, f * ROWS : (f + 1) * ROWS, h * 128 : h * 128 + 128] = col.astype(BF16)
            for k, (r, c) in enumerate(((0, 0), (0, COLS - 1), (ROWS - 1, 0), (ROWS - 1, COLS - 1))):
                p = base + r * COLS + c
                for h in range(2):
                    cb[stage, k, f : f + 1, h * 128 : h * 128 + 128] = wide[h, p : p + 1]

    sends = []

    def send_halo(stage):
        def send(src, dst, device):
            i = len(copies)
            copy = pltpu.make_async_remote_copy(
                src, dst, ssem.at[stage, i], rsem.at[stage, i], device_id=device, device_id_type=MESH
            )
            copy.start()
            copies.append(copy)

        copies = []
        for f in (1, 0):
            send(buf.at[stage, 2 + f, 1 : ROWS + 1], buf.at[stage, f, 1 : ROWS + 1], at(1, 0, 0))
        edges(stage)
        for g, dt in ((1, 0), (0, 1)):
            for dy, dx, kind, a, b in PIECES:
                device = at(dt, dy, dx)
                if kind == "row":
                    send(buf.at[stage, 2:4, a], buf.at[stage, 2 * g : 2 * g + 2, b], device)
                elif kind == "col":
                    send(colp.at[stage, a], colr.at[stage, g, b], device)
                else:
                    send(cb.at[stage, a], cr.at[stage, g, b], device)
        sends.extend(copies)
        near = len(PIECES)
        return copies[2 : near + 2], copies[:2] + copies[near + 2 :]

    def start_plane(stage):
        msg[stage] = compact(sums[...])
        for j, k in PLANE_FAR_FIRST:
            pltpu.make_async_remote_copy(
                msg.at[stage], da.at[stage, j * NCHIP + k - 1], ssem_a.at[stage], rsem_a.at[stage],
                device_id=on_plane(j, k), device_id_type=MESH,
            ).start()

    def start_line(stage):
        everything = da.at[stage]
        pltpu.make_async_copy(everything, everything, rsem_a.at[stage]).wait()
        spans = []
        for j in range(NTA):
            total = msg[stage] if j == 0 else da[stage, j * NCHIP - 1]
            for k in range(1, NCHIP):
                total = total + da[stage, j * NCHIP + k - 1]
            spans.append(total if j == 0 else jnp.where(t >= j, total, 0.0))
        msg3[stage] = jnp.concatenate([spans[0], spans[1], spans[2] + spans[3]], axis=1)
        for i, (c, k) in enumerate(LINE):
            pltpu.make_async_remote_copy(
                msg3.at[stage], db.at[stage, i], ssem_b.at[stage], rsem_b.at[stage],
                device_id=on_line(c, k), device_id_type=MESH,
            ).start()

    def end_line(stage, gain, shift):
        everything = db.at[stage]
        pltpu.make_async_copy(everything, everything, rsem_b.at[stage]).wait()
        total = msg3[stage]
        for i in range(len(LINE)):
            total = total + db[stage, i]
        for i in range(3):
            red[i] = expand(total[:, i * 128 : i * 128 + 128])
        running = []
        for s in (0, 4):
            before = red[2, s : s + 2] + red[2, s + 2 : s + 4]
            row = []
            for i in (1, 0):
                for f in range(2):
                    before = before + red[i, s + 2 * f : s + 2 * f + 2]
                    row.append(before)
            running.append(row)
        for f in range(4):
            count = jnp.maximum((2 * t + f - 1).astype(F32), 1.0) * AREA
            mean = running[0][f] / count
            var = running[1][f] / count - mean * mean
            scale = lax.rsqrt(var + EPS) * gain
            sc[0, 2 * f : 2 * f + 2] = scale
            sc[1, 2 * f : 2 * f + 2] = shift - mean * scale

    def silu(a):
        return 0.5 * a * (1.0 + jnp.tanh(0.5 * a))

    def norm_edges(stage, g):
        for f in range(2):
            for h in range(2):
                lanes = slice(h * 128, h * 128 + 128)
                frame = 2 * g + f
                scale, shift = sc[0, pl.ds(frame * 2 + h, 1)], sc[1, pl.ds(frame * 2 + h, 1)]
                for side in range(2):
                    base = pl.multiple_of((frame * 2 + side) * 32, 32)
                    v = colr[stage, g, side, f * ROWS : (f + 1) * ROWS, lanes].astype(F32)
                    hal[h, pl.ds(base + 8, ROWS)] = silu(v * scale + shift)
                    for place, k in ((7, side), (8 + ROWS, 2 + side)):
                        v = cr[stage, g, k, f : f + 1, lanes]
                        hal[h, pl.ds(base + place, 1)] = silu(v * scale + shift)

    def norm_rows(stage, frame):
        fe = jnp.where((t == 0) & (frame < 2), 2, frame)
        rows = [[sc[i, pl.ds(fe * 2 + h, 1)] for h in range(2)] for i in range(2)]

        def step(r):
            re = jnp.where((r == 0) & (gy == 0), 1, r)
            re = jnp.where((r == ROWS + 1) & (gy == NGY - 1), ROWS, re)
            for h in range(2):
                lanes = slice(h * 128, h * 128 + 128)
                v = buf[stage, fe, re, :, lanes].astype(F32)
                n = silu(v * rows[0][h] + rows[1][h])
                left = hal[h, pl.ds(fe * 64 + 7 + re, 1)]
                right = hal[h, pl.ds(fe * 64 + 39 + re, 1)]
                left = jnp.where(gx == 0, n[0:1], left)
                right = jnp.where(gx == NGX - 1, n[COLS - 1 : COLS], right)
                xs[1, frame, r, :, lanes] = n.astype(BF16)
                xs[0, frame, r, :, lanes] = jnp.where(row_id == 0, left, pltpu.roll(n, 1, 0)).astype(BF16)
                xs[2, frame, r, :, lanes] = jnp.where(
                    row_id == COLS - 1, right, pltpu.roll(n, COLS - 1, 0)
                ).astype(BF16)

        return step

    def normalize(stage, g):
        norm_edges(stage, g)

        def frame_step(f, carry):
            row_step = norm_rows(stage, 2 * g + f)

            def step(r, carry):
                row_step(r)
                return carry

            return lax.fori_loop(0, ROWS + 2, step, carry, unroll=9)

        lax.fori_loop(0, 2, frame_step, 0)

    def fold_weights():
        def step(u, carry):
            a = u // 8
            rows = pl.ds(pl.multiple_of(lax.rem(u, 8) * 32, 32), 32)
            k = [[w2[a * 9 + b * 3 + c, rows].astype(F32) for c in range(3)] for b in range(3)]
            upper = [k[1][c] + k[2][c] for c in range(3)]
            lower = [k[0][c] + k[1][c] for c in range(3)]
            for i, v in enumerate((k[0], upper, lower, k[2])):
                wc[a * 4 + i, rows, 0:CO] = (v[1] + v[2]).astype(BF16)
                wc[a * 4 + i, rows, CO : 2 * CO] = (v[0] + v[1]).astype(BF16)
            for q in range(2):
                we[a * 2 + q, rows, 0:CO] = upper[2 * q].astype(BF16)
                we[a * 2 + q, rows, CO : 2 * CO] = lower[2 * q].astype(BF16)
                wg[a * 2 + q, rows, 0:CO] = k[0][2 * q].astype(BF16)
                wg[a * 2 + q, rows, CO : 2 * CO] = k[2][2 * q].astype(BF16)
            return carry

        lax.fori_loop(0, 24, step, 0)

    def dot(x, w):
        return jnp.dot(x, w, preferred_element_type=F32)

    def flat(piece):
        return piece.reshape(-1, CH)

    def conv_one_row(b):
        total = acc1[...]
        for c in range(3):
            total = total + dot(flat(xs[c, 2:4, b : b + ROWS]), w1[18 + b * 3 + c])
        acc1[...] = total

    def conv_one(a):
        total = acc1[...]
        for b in range(3):
            for c in range(3):
                total = total + dot(flat(xs[c, pl.ds(a, 2), b : b + ROWS]), w1[a * 9 + b * 3 + c])
        acc1[...] = total

    def conv_two(a):
        for p in range(2):
            total = acc2[p]
            for d in range(2):
                total = total + dot(flat(xs[1, pl.ds(a, 2), p + d : p + d + ROWS]), wc[a * 4 + p * 2 + d])
            acc2[p] = total
        for q in range(2):
            acce[q] += dot(flat(xs[2 * q, pl.ds(a, 2), 1 : 1 + ROWS]), we[a * 2 + q])
            accg[q] += dot(flat(xs[2 * q, pl.ds(a, 2)]), wg[a * 2 + q])

    def beside(products, work):
        done = 0
        for i, product in enumerate(products):
            product()
            until = (i + 1) * len(work) // len(products)
            for n in range(done, until):
                work[n]()
            done = until

    def rows_before(stage):
        work = []
        for f in range(2):
            step = norm_rows(stage, f)
            work += [functools.partial(step, r) for r in range(ROWS + 2)]
        return work

    def products_two(a):
        def middle(p):
            total = acc2[p]
            for d in range(2):
                total = total + dot(flat(xs[1, a : a + 2, p + d : p + d + ROWS]), wc[a * 4 + p * 2 + d])
            acc2[p] = total

        def inner(q):
            acce[q] += dot(flat(xs[2 * q, a : a + 2, 1 : 1 + ROWS]), we[a * 2 + q])

        def outer(q):
            accg[q] += dot(flat(xs[2 * q, a : a + 2]), wg[a * 2 + q])

        return [functools.partial(f, i) for f in (middle, inner, outer) for i in range(2)]

    def chain_two():
        def middle(p, f, frames):
            place = slice(f * ROWS * COLS, (f + frames) * ROWS * COLS)
            total = acc2[p, place]
            for a in (1, 0):
                for d in range(2):
                    piece = xs[1, a + f : a + f + frames, p + d : p + d + ROWS]
                    total = total + dot(flat(piece), wc[a * 4 + p * 2 + d])
            acc2[p, place] = total

        def outputs(p, f):
            return [functools.partial(finish, p, f, i) for i in range(ROWS)]

        for q in range(2):
            total = acce[q]
            for a in (1, 0):
                total = total + dot(flat(xs[2 * q, a : a + 2, 1 : 1 + ROWS]), we[a * 2 + q])
            acce[q] = total
            total = accg[q]
            for a in (1, 0):
                total = total + dot(flat(xs[2 * q, a : a + 2]), wg[a * 2 + q])
            accg[q] = total
        middle(0, 0, 2)
        middle(1, 0, 1)
        for work in outputs(0, 0) + outputs(0, 1):
            work()
        middle(1, 1, 1)
        for f in range(2):
            for i, work in enumerate(outputs(1, f)):
                work()
                if i % 4 == 3:
                    store(f, i // 4).start()

    def store(f, part):
        rows = pl.ds(part * 8, 8)
        return pltpu.make_async_copy(ob.at[f, rows], out.at[f, rows], osem.at[f, part])

    def finish(p, f, i):
        slot = i % 8
        place = slice((f * ROWS + i) * COLS, (f * ROWS + i + 1) * COLS)
        row = f * (ROWS + 2) + i + 2 * p
        outer = slice(row * COLS, (row + 1) * COLS)
        for q in range(2):
            v = acc2[p, place, q * CO : (q + 1) * CO] + acce[q, place, p * CO : (p + 1) * CO]
            tmp[slot, pl.ds(q, COLS, stride=2), :] = v + accg[q, outer, p * CO : (p + 1) * CO]
        ob[f, i * 2 + p] = tmp[slot].astype(BF16)

    load_lat.wait()
    take_in(0, lambda f, r: buf[0, 2 + f, 1 + r].astype(F32))
    pl.semaphore_wait(ready, len(senders))
    start_plane(0)
    near, far = send_halo(0)
    for load in loads:
        load.wait()
    start_line(0)
    fold_weights()
    acc1[...] = jnp.zeros_like(acc1)
    end_line(0, prm[0], prm[1])
    for copy in near:
        copy.wait_recv()
    normalize(0, 1)
    for copy in far:
        copy.wait_recv()
    norm_edges(0, 0)
    beside([functools.partial(conv_one_row, b) for b in range(3)], rows_before(0))

    def tap_step(i, carry):
        conv_one(1 - i)
        return carry

    lax.fori_loop(0, 2, tap_step, 0)

    bias = jnp.concatenate([prm[2, 0:1], prm[2, 1:2]], axis=1)

    def block_out(f, r):
        conv = acc1[pl.ds(pl.multiple_of((f * ROWS + r) * COLS, COLS), COLS)]
        v = (buf[0, 2 + f, 1 + r].astype(F32) + conv + bias).astype(BF16)
        buf[1, 2 + f, 1 + r] = v
        return v.astype(F32)

    take_in(1, block_out)
    start_plane(1)
    near, far = send_halo(1)
    start_line(1)
    skip = dot(flat(buf[1, 2:4, 1 : ROWS + 1]), ws[...]) + b2[...]
    for p in range(2):
        for q in range(2):
            acc2[p, :, q * CO : (q + 1) * CO] = skip
    acce[...] = jnp.zeros_like(acce)
    accg[...] = jnp.zeros_like(accg)
    end_line(1, prm[3], prm[4])
    for copy in near:
        copy.wait_recv()
    normalize(1, 1)
    for copy in far:
        copy.wait_recv()
    norm_edges(1, 0)
    beside(products_two(2), rows_before(1))
    chain_two()

    for copy in sends:
        copy.wait_send()
    for stage in range(2):
        pltpu.make_async_copy(da.at[stage], da.at[stage], ssem_a.at[stage]).wait()
        pltpu.make_async_copy(db.at[stage], db.at[stage], ssem_b.at[stage]).wait()
    for f in range(2):
        for part in range(4):
            store(f, part).wait()


def on_device(
    latents, gain_one, shift_one, weight_one, bias_one, gain_two, shift_two, weight_two, weight_skip, bias_two
):
    vmem = pltpu.VMEM
    dma = pltpu.SemaphoreType.DMA
    n_halo = 2 * len(PIECES) + 2
    halves = lambda v: v.reshape(2, 128)
    return pl.pallas_call(
        kernel,
        out_shape=jax.ShapeDtypeStruct((2, 2 * ROWS, 2 * COLS, CO), BF16),
        in_specs=[pl.BlockSpec(memory_space=pl.ANY)] * 10,
        out_specs=pl.BlockSpec(memory_space=pl.ANY),
        scratch_shapes=[
            vmem((2, 4, ROWS + 2, COLS, CH), BF16),
            vmem((2, 2, 2 * ROWS, CH), BF16),
            vmem((2, 2, 2, 2 * ROWS, CH), BF16),
            vmem((2, 4, 2, CH), F32),
            vmem((2, 2, 4, 2, CH), F32),
            vmem((2, 2 * ROWS * COLS, 128), F32),
            vmem((3, 4, ROWS + 2, COLS, CH), BF16),
            vmem((2, 8 * 32, 128), F32),
            vmem((8, 128), F32),
            vmem((3, 8, 128), F32),
            vmem((2, 8, 128), F32),
            vmem((27, CH, CH), BF16),
            vmem((27, CH, CO), BF16),
            vmem((12, CH, 2 * CO), BF16),
            vmem((6, CH, 2 * CO), BF16),
            vmem((6, CH, 2 * CO), BF16),
            vmem((CH, CO), BF16),
            vmem((5, 2, 128), F32),
            vmem((1, CO), F32),
            vmem((2 * ROWS * COLS, CH), F32),
            vmem((2, 2 * ROWS * COLS, 2 * CO), F32),
            vmem((2, 2 * ROWS * COLS, 2 * CO), F32),
            vmem((2, 2 * (ROWS + 2) * COLS, 2 * CO), F32),
            vmem((8, 2 * COLS, CO), F32),
            vmem((2, 2 * ROWS, 2 * COLS, CO), BF16),
            vmem((2, 1, 128), F32),
            vmem((2, 1, 384), F32),
            vmem((2, len(PLANE), 1, 128), F32),
            vmem((2, len(LINE), 1, 384), F32),
            dma((2, n_halo)),
            dma((2, n_halo)),
            dma((2,)),
            dma((2,)),
            dma((2,)),
            dma((2,)),
            dma((10,)),
            dma((2, 4)),
        ],
        compiler_params=pltpu.CompilerParams(
            collective_id=0, has_side_effects=True, vmem_limit_bytes=62 << 20
        ),
    )(
        latents,
        weight_one.reshape(27, CH, CH),
        weight_two.reshape(27, CH, CO),
        weight_skip,
        halves(gain_one),
        halves(shift_one),
        halves(bias_one),
        halves(gain_two),
        halves(shift_two),
        bias_two.reshape(1, CO),
    )


def solution(mesh):
    in_specs = (P("ta", "gy", "gx", None),) + (P(),) * 9
    return jax.shard_map(
        on_device, mesh=mesh, in_specs=in_specs, out_specs=P("ta", "gy", "gx", None), check_vma=False
    )
```

```python
import functools

import jax
import jax.numpy as jnp
from jax import lax
from jax.experimental import pallas as pl
from jax.experimental.pallas import tpu as pltpu
from jax.sharding import PartitionSpec as P

MESH = pl.DeviceIdType.MESH
F32 = jnp.float32
BF16 = jnp.bfloat16
EPS = 1e-06

NTA, NCHIP, NGX = 4, 4, 8
NGY = 2 * NCHIP
ROWS, COLS, CH, CO = 16, 16, 256, 128
AREA = float(NGY * ROWS * NGX * COLS * (CH // 32))

PLANE = [(j, k) for j in range(NTA) for k in range(NCHIP) if (j, k) != (0, 0)]
PLANE_FAR_FIRST = sorted(PLANE, key=lambda p: -(min(p[0], NTA - p[0]) + min(p[1], NCHIP - p[1])))
LINE = [(c, k) for k in (4, 3, -3, 2, -2, 1, -1, 0) for c in (1, 0) if (c, k) != (0, 0)]

PIECES = [
    (-1, 0, "row", 1, ROWS + 1),
    (1, 0, "row", ROWS, 0),
    (0, -1, "col", 0, 1),
    (0, 1, "col", 1, 0),
    (-1, -1, "corner", 0, 3),
    (-1, 1, "corner", 1, 2),
    (1, -1, "corner", 2, 1),
    (1, 1, "corner", 3, 0),
]


def wrap(value, size):
    return lax.rem(value + size, size)


def kernel(
    lat, w1h, w2h, wsh, g1h, s1h, b1h, g2h, s2h, b2h, out,
    buf, colp, colr, cb, cr, wide, xs, hal, sums, sc, w1, w2, wc, we, wg, ws, prm, b2,
    acc1, acc2, acce, accg, tmp, ob,
    msg, msg2, da, db, ssem, rsem, ssem_a, rsem_a, ssem_b, rsem_b, lsem, osem,
):
    t = lax.axis_index("ta")
    gy = lax.axis_index("gy")
    gx = lax.axis_index("gx")
    chip, core = gy // 2, lax.rem(gy, 2)

    def at(dt, dy, dx):
        return (wrap(t + dt, NTA), wrap(gy + dy, NGY), wrap(gx + dx, NGX))

    def on_line(c, k):
        return (t, chip * 2 + (1 - core if c else core), wrap(gx + k, NGX))

    def on_plane(j, k):
        return (wrap(t + j, NTA), wrap(chip + k, NCHIP) * 2 + core, gx)

    ready = pltpu.get_barrier_semaphore()
    senders = [on_plane(j, k) for j, k in PLANE_FAR_FIRST] + [on_line(c, k) for c, k in LINE]
    senders += [at(0, dy, dx) for dy, dx, _, _, _ in PIECES]
    senders += [at(-1, 0, 0)] + [at(-1, dy, dx) for dy, dx, _, _, _ in PIECES]
    load_lat = pltpu.make_async_copy(lat, buf.at[0, 2:4, 1 : ROWS + 1], lsem.at[0])
    load_lat.start()
    for device in senders:
        pl.semaphore_signal(ready, inc=1, device_id=device, device_id_type=MESH)
    loads = [
        pltpu.make_async_copy(src, dst, lsem.at[i + 1])
        for i, (src, dst) in enumerate(
            [(w2h, w2), (wsh, ws), (g1h, prm.at[0]), (s1h, prm.at[1]), (b1h, prm.at[2]),
             (g2h, prm.at[3]), (s2h, prm.at[4]), (b2h, b2), (w1h, w1)]
        )
    ]
    for load in loads:
        load.start()

    lane = lax.broadcasted_iota(jnp.int32, (8, 128), 1)
    pick = lax.rem(lane, 8) == lax.broadcasted_iota(jnp.int32, (8, 128), 0)
    row_id = lax.broadcasted_iota(jnp.int32, (COLS, 128), 0)

    def group_sum(v):
        for d in (1, 2, 4):
            v = v + jnp.where((lane & d) != 0, pltpu.roll(v, d, 1), pltpu.roll(v, 128 - d, 1))
        return v

    def compact(v):
        return jnp.sum(jnp.where(pick, group_sum(v), 0.0), axis=0, keepdims=True)

    def expand(row):
        return group_sum(jnp.where(pick, jnp.broadcast_to(row, (8, 128)), 0.0))

    def take_in(stage, block):
        for f in range(2):

            def step(r, carry):
                s, q = carry
                v = block(f, r)
                place = pl.ds(pl.multiple_of((f * ROWS + r) * COLS, COLS), COLS)
                for h in range(2):
                    wide[h, place] = v[:, h * 128 : h * 128 + 128]
                return s + v, q + v * v

            zero = jnp.zeros((COLS, CH), F32)
            s, q = lax.fori_loop(0, ROWS, step, (zero, zero), unroll=4)
            s = jnp.sum(s, axis=0, keepdims=True)
            q = jnp.sum(q, axis=0, keepdims=True)
            for h in range(2):
                lanes = slice(h * 128, h * 128 + 128)
                sums[f * 2 + h : f * 2 + h + 1] = s[:, lanes]
                sums[4 + f * 2 + h : 5 + f * 2 + h] = q[:, lanes]

    def edges(stage):
        for f in range(2):
            base = f * ROWS * COLS
            for side, c in ((0, 0), (1, COLS - 1)):
                for h in range(2):
                    col = wide.at[h][pl.ds(base + c, ROWS, stride=COLS), :]
                    colp[stage, side, f * ROWS : (f + 1) * ROWS, h * 128 : h * 128 + 128] = col.astype(BF16)
            for k, (r, c) in enumerate(((0, 0), (0, COLS - 1), (ROWS - 1, 0), (ROWS - 1, COLS - 1))):
                p = base + r * COLS + c
                for h in range(2):
                    cb[stage, k, f : f + 1, h * 128 : h * 128 + 128] = wide[h, p : p + 1]

    sends = []

    def send_halo(stage):
        def send(src, dst, device):
            i = len(copies)
            copy = pltpu.make_async_remote_copy(
                src, dst, ssem.at[stage, i], rsem.at[stage, i], device_id=device, device_id_type=MESH
            )
            copy.start()
            copies.append(copy)

        copies = []
        for f in (1, 0):
            send(buf.at[stage, 2 + f, 1 : ROWS + 1], buf.at[stage, f, 1 : ROWS + 1], at(1, 0, 0))
        edges(stage)
        for g, dt in ((1, 0), (0, 1)):
            for dy, dx, kind, a, b in PIECES:
                device = at(dt, dy, dx)
                if kind == "row":
                    send(buf.at[stage, 2:4, a], buf.at[stage, 2 * g : 2 * g + 2, b], device)
                elif kind == "col":
                    send(colp.at[stage, a], colr.at[stage, g, b], device)
                else:
                    send(cb.at[stage, a], cr.at[stage, g, b], device)
        sends.extend(copies)
        near = len(PIECES)
        return copies[2 : near + 2], copies[:2] + copies[near + 2 :]

    def start_plane(stage):
        msg[stage] = compact(sums[...])
        for j, k in PLANE_FAR_FIRST:
            pltpu.make_async_remote_copy(
                msg.at[stage], da.at[stage, j * NCHIP + k - 1], ssem_a.at[stage], rsem_a.at[stage],
                device_id=on_plane(j, k), device_id_type=MESH,
            ).start()

    def start_line(stage):
        everything = da.at[stage]
        pltpu.make_async_copy(everything, everything, rsem_a.at[stage]).wait()
        spans = []
        for j in range(NTA):
            total = msg[stage] if j == 0 else da[stage, j * NCHIP - 1]
            for k in range(1, NCHIP):
                total = total + da[stage, j * NCHIP + k - 1]
            spans.append(total if j == 0 else jnp.where(t >= j, total, 0.0))
        second = (lane[0:1] & 2) != 0
        up = [pltpu.roll(v, 2, 1) for v in (spans[0], spans[1], spans[2] + spans[3])]
        own, before = [v + jnp.where(second, u, 0.0) for v, u in zip(spans[:2], up)]
        pair = spans[1] + jnp.where(second, up[1], pltpu.roll(spans[1], 126, 1))
        older = spans[2] + spans[3]
        older = older + jnp.where(second, up[2], pltpu.roll(older, 126, 1))
        msg2[stage] = jnp.concatenate([before + older, own + (pair + older)], axis=1)
        for i, (c, k) in enumerate(LINE):
            pltpu.make_async_remote_copy(
                msg2.at[stage], db.at[stage, i], ssem_b.at[stage], rsem_b.at[stage],
                device_id=on_line(c, k), device_id_type=MESH,
            ).start()

    def end_line(stage, gain, shift):
        everything = db.at[stage]
        pltpu.make_async_copy(everything, everything, rsem_b.at[stage]).wait()
        total = msg2[stage]
        for i in range(len(LINE)):
            total = total + db[stage, i]
        frame = lax.broadcasted_iota(jnp.int32, (4, 128), 0) // 2
        gain = jnp.concatenate([gain, gain], axis=0)
        shift = jnp.concatenate([shift, shift], axis=0)
        for g in range(2):
            running = expand(total[:, g * 128 : g * 128 + 128])
            count = jnp.maximum((2 * t + (2 * g - 1) + frame).astype(F32), 1.0) * AREA
            mean = running[0:4] / count
            var = running[4:8] / count - mean * mean
            scale = lax.rsqrt(var + EPS) * gain
            sc[0, 4 * g : 4 * g + 4] = scale
            sc[1, 4 * g : 4 * g + 4] = shift - mean * scale

    def silu(a):
        return 0.5 * a * (1.0 + jnp.tanh(0.5 * a))

    def norm_edges(stage, g):
        for f in range(2):
            for h in range(2):
                lanes = slice(h * 128, h * 128 + 128)
                frame = 2 * g + f
                scale, shift = sc[0, pl.ds(frame * 2 + h, 1)], sc[1, pl.ds(frame * 2 + h, 1)]
                for side in range(2):
                    base = pl.multiple_of((frame * 2 + side) * 32, 32)
                    v = colr[stage, g, side, f * ROWS : (f + 1) * ROWS, lanes].astype(F32)
                    hal[h, pl.ds(base + 8, ROWS)] = silu(v * scale + shift)
                    for place, k in ((7, side), (8 + ROWS, 2 + side)):
                        v = cr[stage, g, k, f : f + 1, lanes]
                        hal[h, pl.ds(base + place, 1)] = silu(v * scale + shift)

    def norm_rows(stage, frame):
        fe = jnp.where((t == 0) & (frame < 2), 2, frame)
        rows = [[sc[i, pl.ds(fe * 2 + h, 1)] for h in range(2)] for i in range(2)]

        def step(r):
            re = jnp.where((r == 0) & (gy == 0), 1, r)
            re = jnp.where((r == ROWS + 1) & (gy == NGY - 1), ROWS, re)
            for h in range(2):
                lanes = slice(h * 128, h * 128 + 128)
                v = buf[stage, fe, re, :, lanes].astype(F32)
                n = silu(v * rows[0][h] + rows[1][h])
                left = hal[h, pl.ds(fe * 64 + 7 + re, 1)]
                right = hal[h, pl.ds(fe * 64 + 39 + re, 1)]
                left = jnp.where(gx == 0, n[0:1], left)
                right = jnp.where(gx == NGX - 1, n[COLS - 1 : COLS], right)
                xs[1, frame, r, :, lanes] = n.astype(BF16)
                xs[0, frame, r, :, lanes] = jnp.where(row_id == 0, left, pltpu.roll(n, 1, 0)).astype(BF16)
                xs[2, frame, r, :, lanes] = jnp.where(
                    row_id == COLS - 1, right, pltpu.roll(n, COLS - 1, 0)
                ).astype(BF16)

        return step

    def normalize(stage, g):
        norm_edges(stage, g)

        def frame_step(f, carry):
            row_step = norm_rows(stage, 2 * g + f)

            def step(r, carry):
                row_step(r)
                return carry

            return lax.fori_loop(0, ROWS + 2, step, carry, unroll=9)

        lax.fori_loop(0, 2, frame_step, 0)

    def fold_weights():
        def step(u, carry):
            a = u // 8
            rows = pl.ds(pl.multiple_of(lax.rem(u, 8) * 32, 32), 32)
            k = [[w2[a * 9 + b * 3 + c, rows].astype(F32) for c in range(3)] for b in range(3)]
            upper = [k[1][c] + k[2][c] for c in range(3)]
            lower = [k[0][c] + k[1][c] for c in range(3)]
            for i, v in enumerate((k[0], upper, lower, k[2])):
                wc[a * 4 + i, rows, 0:CO] = (v[1] + v[2]).astype(BF16)
                wc[a * 4 + i, rows, CO : 2 * CO] = (v[0] + v[1]).astype(BF16)
            for q in range(2):
                we[a * 2 + q, rows, 0:CO] = upper[2 * q].astype(BF16)
                we[a * 2 + q, rows, CO : 2 * CO] = lower[2 * q].astype(BF16)
                wg[a * 2 + q, rows, 0:CO] = k[0][2 * q].astype(BF16)
                wg[a * 2 + q, rows, CO : 2 * CO] = k[2][2 * q].astype(BF16)
            return carry

        lax.fori_loop(0, 24, step, 0)

    def dot(x, w):
        return jnp.dot(x, w, preferred_element_type=F32)

    def flat(piece):
        return piece.reshape(-1, CH)

    def conv_one_row(b):
        total = acc1[...]
        for c in range(3):
            total = total + dot(flat(xs[c, 2:4, b : b + ROWS]), w1[18 + b * 3 + c])
        acc1[...] = total

    def conv_one(a):
        total = acc1[...]
        for b in range(3):
            for c in range(3):
                total = total + dot(flat(xs[c, pl.ds(a, 2), b : b + ROWS]), w1[a * 9 + b * 3 + c])
        acc1[...] = total

    def conv_two(a):
        for p in range(2):
            total = acc2[p]
            for d in range(2):
                total = total + dot(flat(xs[1, pl.ds(a, 2), p + d : p + d + ROWS]), wc[a * 4 + p * 2 + d])
            acc2[p] = total
        for q in range(2):
            acce[q] += dot(flat(xs[2 * q, pl.ds(a, 2), 1 : 1 + ROWS]), we[a * 2 + q])
            accg[q] += dot(flat(xs[2 * q, pl.ds(a, 2)]), wg[a * 2 + q])

    def beside(products, work):
        done = 0
        for i, product in enumerate(products):
            product()
            until = (i + 1) * len(work) // len(products)
            for n in range(done, until):
                work[n]()
            done = until

    def rows_before(stage):
        work = []
        for f in range(2):
            step = norm_rows(stage, f)
            work += [functools.partial(step, r) for r in range(ROWS + 2)]
        return work

    def products_two(a):
        def middle(p):
            total = acc2[p]
            for d in range(2):
                total = total + dot(flat(xs[1, a : a + 2, p + d : p + d + ROWS]), wc[a * 4 + p * 2 + d])
            acc2[p] = total

        def inner(q):
            acce[q] += dot(flat(xs[2 * q, a : a + 2, 1 : 1 + ROWS]), we[a * 2 + q])

        def outer(q):
            accg[q] += dot(flat(xs[2 * q, a : a + 2]), wg[a * 2 + q])

        return [functools.partial(f, i) for f in (middle, inner, outer) for i in range(2)]

    def chain_two():
        def middle(p, f, frames):
            place = slice(f * ROWS * COLS, (f + frames) * ROWS * COLS)
            total = acc2[p, place]
            for a in (1, 0):
                for d in range(2):
                    piece = xs[1, a + f : a + f + frames, p + d : p + d + ROWS]
                    total = total + dot(flat(piece), wc[a * 4 + p * 2 + d])
            acc2[p, place] = total

        for q in range(2):
            total = acce[q]
            for a in (1, 0):
                total = total + dot(flat(xs[2 * q, a : a + 2, 1 : 1 + ROWS]), we[a * 2 + q])
            acce[q] = total
            total = accg[q]
            for a in (1, 0):
                total = total + dot(flat(xs[2 * q, a : a + 2]), wg[a * 2 + q])
            accg[q] = total
        middle(0, 0, 2)
        middle(1, 0, 2)

        def step(u, carry):
            f, part = u // 4, lax.rem(u, 4)
            for n in range(4):
                for p in range(2):
                    finish(p, f, part * 4 + n, 2 * n + p)
            store(f, part).start()
            return carry

        lax.fori_loop(0, 8, step, 0)

    def store(f, part):
        rows = pl.ds(part * 8, 8)
        return pltpu.make_async_copy(ob.at[f, rows], out.at[f, rows], osem.at[f, part])

    def finish(p, f, i, slot):
        place = pl.ds(pl.multiple_of((f * ROWS + i) * COLS, COLS), COLS)
        outer = pl.ds(pl.multiple_of((f * (ROWS + 2) + i + 2 * p) * COLS, COLS), COLS)
        for q in range(2):
            v = acc2[p, place, q * CO : (q + 1) * CO] + acce[q, place, p * CO : (p + 1) * CO]
            tmp[slot, pl.ds(q, COLS, stride=2), :] = v + accg[q, outer, p * CO : (p + 1) * CO]
        ob[f, i * 2 + p] = tmp[slot].astype(BF16)

    load_lat.wait()
    take_in(0, lambda f, r: buf[0, 2 + f, 1 + r].astype(F32))
    pl.semaphore_wait(ready, len(senders))
    start_plane(0)
    near, far = send_halo(0)
    for load in loads:
        load.wait()
    start_line(0)
    fold_weights()
    acc1[...] = jnp.zeros_like(acc1)
    end_line(0, prm[0], prm[1])
    for copy in near:
        copy.wait_recv()
    normalize(0, 1)
    for copy in far:
        copy.wait_recv()
    norm_edges(0, 0)
    beside([functools.partial(conv_one_row, b) for b in range(3)], rows_before(0))

    def tap_step(i, carry):
        conv_one(1 - i)
        return carry

    lax.fori_loop(0, 2, tap_step, 0)

    bias = jnp.concatenate([prm[2, 0:1], prm[2, 1:2]], axis=1)

    def block_out(f, r):
        conv = acc1[pl.ds(pl.multiple_of((f * ROWS + r) * COLS, COLS), COLS)]
        v = (buf[0, 2 + f, 1 + r].astype(F32) + conv + bias).astype(BF16)
        buf[1, 2 + f, 1 + r] = v
        return v.astype(F32)

    take_in(1, block_out)
    start_plane(1)
    near, far = send_halo(1)
    start_line(1)
    skip = dot(flat(buf[1, 2:4, 1 : ROWS + 1]), ws[...]) + b2[...]
    for p in range(2):
        for q in range(2):
            acc2[p, :, q * CO : (q + 1) * CO] = skip
    acce[...] = jnp.zeros_like(acce)
    accg[...] = jnp.zeros_like(accg)
    end_line(1, prm[3], prm[4])
    for copy in near:
        copy.wait_recv()
    normalize(1, 1)
    for copy in far:
        copy.wait_recv()
    norm_edges(1, 0)
    beside(products_two(2), rows_before(1))
    chain_two()

    for copy in sends:
        copy.wait_send()
    for stage in range(2):
        pltpu.make_async_copy(da.at[stage], da.at[stage], ssem_a.at[stage]).wait()
        pltpu.make_async_copy(db.at[stage], db.at[stage], ssem_b.at[stage]).wait()
    for f in range(2):
        for part in range(4):
            store(f, part).wait()


def on_device(
    latents, gain_one, shift_one, weight_one, bias_one, gain_two, shift_two, weight_two, weight_skip, bias_two
):
    vmem = pltpu.VMEM
    dma = pltpu.SemaphoreType.DMA
    n_halo = 2 * len(PIECES) + 2
    halves = lambda v: v.reshape(2, 128)
    return pl.pallas_call(
        kernel,
        out_shape=jax.ShapeDtypeStruct((2, 2 * ROWS, 2 * COLS, CO), BF16),
        in_specs=[pl.BlockSpec(memory_space=pl.ANY)] * 10,
        out_specs=pl.BlockSpec(memory_space=pl.ANY),
        scratch_shapes=[
            vmem((2, 4, ROWS + 2, COLS, CH), BF16),
            vmem((2, 2, 2 * ROWS, CH), BF16),
            vmem((2, 2, 2, 2 * ROWS, CH), BF16),
            vmem((2, 4, 2, CH), F32),
            vmem((2, 2, 4, 2, CH), F32),
            vmem((2, 2 * ROWS * COLS, 128), F32),
            vmem((3, 4, ROWS + 2, COLS, CH), BF16),
            vmem((2, 8 * 32, 128), F32),
            vmem((8, 128), F32),
            vmem((2, 8, 128), F32),
            vmem((27, CH, CH), BF16),
            vmem((27, CH, CO), BF16),
            vmem((12, CH, 2 * CO), BF16),
            vmem((6, CH, 2 * CO), BF16),
            vmem((6, CH, 2 * CO), BF16),
            vmem((CH, CO), BF16),
            vmem((5, 2, 128), F32),
            vmem((1, CO), F32),
            vmem((2 * ROWS * COLS, CH), F32),
            vmem((2, 2 * ROWS * COLS, 2 * CO), F32),
            vmem((2, 2 * ROWS * COLS, 2 * CO), F32),
            vmem((2, 2 * (ROWS + 2) * COLS, 2 * CO), F32),
            vmem((8, 2 * COLS, CO), F32),
            vmem((2, 2 * ROWS, 2 * COLS, CO), BF16),
            vmem((2, 1, 128), F32),
            vmem((2, 1, 256), F32),
            vmem((2, len(PLANE), 1, 128), F32),
            vmem((2, len(LINE), 1, 256), F32),
            dma((2, n_halo)),
            dma((2, n_halo)),
            dma((2,)),
            dma((2,)),
            dma((2,)),
            dma((2,)),
            dma((10,)),
            dma((2, 4)),
        ],
        compiler_params=pltpu.CompilerParams(
            collective_id=0, has_side_effects=True, vmem_limit_bytes=62 << 20
        ),
    )(
        latents,
        weight_one.reshape(27, CH, CH),
        weight_two.reshape(27, CH, CO),
        weight_skip,
        halves(gain_one),
        halves(shift_one),
        halves(bias_one),
        halves(gain_two),
        halves(shift_two),
        bias_two.reshape(1, CO),
    )


def solution(mesh):
    in_specs = (P("ta", "gy", "gx", None),) + (P(),) * 9
    return jax.shard_map(
        on_device, mesh=mesh, in_specs=in_specs, out_specs=P("ta", "gy", "gx", None), check_vma=False
    )
```

```python
import functools

import jax
import jax.numpy as jnp
from jax import lax
from jax.experimental import pallas as pl
from jax.experimental.pallas import tpu as pltpu
from jax.sharding import PartitionSpec as P

MESH = pl.DeviceIdType.MESH
F32 = jnp.float32
BF16 = jnp.bfloat16
EPS = 1e-06

NTA, NCHIP, NGX = 4, 4, 8
NGY = 2 * NCHIP
ROWS, COLS, CH, CO = 16, 16, 256, 128
AREA = float(NGY * ROWS * NGX * COLS * (CH // 32))

PLANE = [(j, k) for j in range(NTA) for k in range(NCHIP) if (j, k) != (0, 0)]
PLANE_FAR_FIRST = sorted(PLANE, key=lambda p: -(min(p[0], NTA - p[0]) + min(p[1], NCHIP - p[1])))
LINE = [(c, k) for k in (4, 3, -3, 2, -2, 1, -1, 0) for c in (1, 0) if (c, k) != (0, 0)]

PIECES = [
    (-1, 0, "row", 1, ROWS + 1),
    (1, 0, "row", ROWS, 0),
    (0, -1, "col", 0, 1),
    (0, 1, "col", 1, 0),
    (-1, -1, "corner", 0, 3),
    (-1, 1, "corner", 1, 2),
    (1, -1, "corner", 2, 1),
    (1, 1, "corner", 3, 0),
]


def wrap(value, size):
    return lax.rem(value + size, size)


def kernel(
    lat, w1h, w2h, wsh, g1h, s1h, b1h, g2h, s2h, b2h, out,
    buf, colp, colr, cb, cr, wide, xs, hal, sums, red, sc, w1, w2, wc, we, wg, ws, prm, b2,
    acc1, acc2, acce, accg, tmp, ob,
    msg, msg3, da, db, ssem, rsem, ssem_a, rsem_a, ssem_b, rsem_b, lsem, osem,
):
    t = lax.axis_index("ta")
    gy = lax.axis_index("gy")
    gx = lax.axis_index("gx")
    chip, core = gy // 2, lax.rem(gy, 2)

    def at(dt, dy, dx):
        return (wrap(t + dt, NTA), wrap(gy + dy, NGY), wrap(gx + dx, NGX))

    def on_line(c, k):
        return (t, chip * 2 + (1 - core if c else core), wrap(gx + k, NGX))

    def on_plane(j, k):
        return (wrap(t + j, NTA), wrap(chip + k, NCHIP) * 2 + core, gx)

    ready = pltpu.get_barrier_semaphore()
    senders = [on_plane(j, k) for j, k in PLANE_FAR_FIRST] + [on_line(c, k) for c, k in LINE]
    senders += [at(0, dy, dx) for dy, dx, _, _, _ in PIECES]
    senders += [at(-1, 0, 0)] + [at(-1, dy, dx) for dy, dx, _, _, _ in PIECES]
    load_lat = pltpu.make_async_copy(lat, buf.at[0, 2:4, 1 : ROWS + 1], lsem.at[0])
    load_lat.start()
    for device in senders:
        pl.semaphore_signal(ready, inc=1, device_id=device, device_id_type=MESH)
    loads = [
        pltpu.make_async_copy(src, dst, lsem.at[i + 1])
        for i, (src, dst) in enumerate(
            [(w2h, w2), (wsh, ws), (g1h, prm.at[0]), (s1h, prm.at[1]), (b1h, prm.at[2]),
             (g2h, prm.at[3]), (s2h, prm.at[4]), (b2h, b2), (w1h, w1)]
        )
    ]
    for load in loads:
        load.start()

    lane = lax.broadcasted_iota(jnp.int32, (8, 128), 1)
    pick = lax.rem(lane, 8) == lax.broadcasted_iota(jnp.int32, (8, 128), 0)
    row_id = lax.broadcasted_iota(jnp.int32, (COLS, 128), 0)

    def group_sum(v):
        for d in (1, 2, 4):
            v = v + jnp.where((lane & d) != 0, pltpu.roll(v, d, 1), pltpu.roll(v, 128 - d, 1))
        return v

    def compact(v):
        return jnp.sum(jnp.where(pick, group_sum(v), 0.0), axis=0, keepdims=True)

    def expand(row):
        return group_sum(jnp.where(pick, jnp.broadcast_to(row, (8, 128)), 0.0))

    def take_in(stage, block):
        for f in range(2):

            def step(r, carry):
                s, q = carry
                v = block(f, r)
                place = pl.ds(pl.multiple_of((f * ROWS + r) * COLS, COLS), COLS)
                for h in range(2):
                    wide[h, place] = v[:, h * 128 : h * 128 + 128]
                return s + v, q + v * v

            zero = jnp.zeros((COLS, CH), F32)
            s, q = lax.fori_loop(0, ROWS, step, (zero, zero), unroll=8)
            s = jnp.sum(s, axis=0, keepdims=True)
            q = jnp.sum(q, axis=0, keepdims=True)
            for h in range(2):
                lanes = slice(h * 128, h * 128 + 128)
                sums[f * 2 + h : f * 2 + h + 1] = s[:, lanes]
                sums[4 + f * 2 + h : 5 + f * 2 + h] = q[:, lanes]

    def edges(stage):
        for f in range(2):
            base = f * ROWS * COLS
            for side, c in ((0, 0), (1, COLS - 1)):
                for h in range(2):
                    col = wide.at[h][pl.ds(base + c, ROWS, stride=COLS), :]
                    colp[stage, side, f * ROWS : (f + 1) * ROWS, h * 128 : h * 128 + 128] = col.astype(BF16)
            for k, (r, c) in enumerate(((0, 0), (0, COLS - 1), (ROWS - 1, 0), (ROWS - 1, COLS - 1))):
                p = base + r * COLS + c
                for h in range(2):
                    cb[stage, k, f : f + 1, h * 128 : h * 128 + 128] = wide[h, p : p + 1]

    sends = []

    def send_halo(stage):
        def send(src, dst, device):
            i = len(copies)
            copy = pltpu.make_async_remote_copy(
                src, dst, ssem.at[stage, i], rsem.at[stage, i], device_id=device, device_id_type=MESH
            )
            copy.start()
            copies.append(copy)

        copies = []
        for f in (1, 0):
            send(buf.at[stage, 2 + f, 1 : ROWS + 1], buf.at[stage, f, 1 : ROWS + 1], at(1, 0, 0))
        edges(stage)
        for g, dt in ((1, 0), (0, 1)):
            for dy, dx, kind, a, b in PIECES:
                device = at(dt, dy, dx)
                if kind == "row":
                    send(buf.at[stage, 2:4, a], buf.at[stage, 2 * g : 2 * g + 2, b], device)
                elif kind == "col":
                    send(colp.at[stage, a], colr.at[stage, g, b], device)
                else:
                    send(cb.at[stage, a], cr.at[stage, g, b], device)
        sends.extend(copies)
        near = len(PIECES)
        return copies[2 : near + 2], copies[:2] + copies[near + 2 :]

    def start_plane(stage):
        msg[stage] = compact(sums[...])
        for j, k in PLANE_FAR_FIRST:
            pltpu.make_async_remote_copy(
                msg.at[stage], da.at[stage, j * NCHIP + k - 1], ssem_a.at[stage], rsem_a.at[stage],
                device_id=on_plane(j, k), device_id_type=MESH,
            ).start()

    def start_line(stage):
        everything = da.at[stage]
        pltpu.make_async_copy(everything, everything, rsem_a.at[stage]).wait()
        spans = []
        for j in range(NTA):
            total = msg[stage] if j == 0 else da[stage, j * NCHIP - 1]
            for k in range(1, NCHIP):
                total = total + da[stage, j * NCHIP + k - 1]
            spans.append(total if j == 0 else jnp.where(t >= j, total, 0.0))
        msg3[stage] = jnp.concatenate([spans[0], spans[1], spans[2] + spans[3]], axis=1)
        for i, (c, k) in enumerate(LINE):
            pltpu.make_async_remote_copy(
                msg3.at[stage], db.at[stage, i], ssem_b.at[stage], rsem_b.at[stage],
                device_id=on_line(c, k), device_id_type=MESH,
            ).start()

    def end_line(stage, gain, shift):
        everything = db.at[stage]
        pltpu.make_async_copy(everything, everything, rsem_b.at[stage]).wait()
        total = msg3[stage]
        for i in range(len(LINE)):
            total = total + db[stage, i]
        for i in range(3):
            red[i] = expand(total[:, i * 128 : i * 128 + 128])
        running = []
        for s in (0, 4):
            before = red[2, s : s + 2] + red[2, s + 2 : s + 4]
            row = []
            for i in (1, 0):
                for f in range(2):
                    before = before + red[i, s + 2 * f : s + 2 * f + 2]
                    row.append(before)
            running.append(row)
        for f in range(4):
            count = jnp.maximum((2 * t + f - 1).astype(F32), 1.0) * AREA
            mean = running[0][f] / count
            var = running[1][f] / count - mean * mean
            scale = lax.rsqrt(var + EPS) * gain
            sc[0, 2 * f : 2 * f + 2] = scale
            sc[1, 2 * f : 2 * f + 2] = shift - mean * scale

    def silu(a):
        return 0.5 * a * (1.0 + jnp.tanh(0.5 * a))

    def norm_edges(stage, g):
        for f in range(2):
            for h in range(2):
                lanes = slice(h * 128, h * 128 + 128)
                frame = 2 * g + f
                scale, shift = sc[0, pl.ds(frame * 2 + h, 1)], sc[1, pl.ds(frame * 2 + h, 1)]
                for side in range(2):
                    base = pl.multiple_of((frame * 2 + side) * 32, 32)
                    v = colr[stage, g, side, f * ROWS : (f + 1) * ROWS, lanes].astype(F32)
                    hal[h, pl.ds(base + 8, ROWS)] = silu(v * scale + shift)
                    for place, k in ((7, side), (8 + ROWS, 2 + side)):
                        v = cr[stage, g, k, f : f + 1, lanes]
                        hal[h, pl.ds(base + place, 1)] = silu(v * scale + shift)

    def norm_rows(stage, frame):
        fe = jnp.where((t == 0) & (frame < 2), 2, frame)
        rows = [[sc[i, pl.ds(fe * 2 + h, 1)] for h in range(2)] for i in range(2)]

        def step(r):
            re = jnp.where((r == 0) & (gy == 0), 1, r)
            re = jnp.where((r == ROWS + 1) & (gy == NGY - 1), ROWS, re)
            for h in range(2):
                lanes = slice(h * 128, h * 128 + 128)
                v = buf[stage, fe, re, :, lanes].astype(F32)
                n = silu(v * rows[0][h] + rows[1][h])
                left = hal[h, pl.ds(fe * 64 + 7 + re, 1)]
                right = hal[h, pl.ds(fe * 64 + 39 + re, 1)]
                left = jnp.where(gx == 0, n[0:1], left)
                right = jnp.where(gx == NGX - 1, n[COLS - 1 : COLS], right)
                xs[1, frame, r, :, lanes] = n.astype(BF16)
                xs[0, frame, r, :, lanes] = jnp.where(row_id == 0, left, pltpu.roll(n, 1, 0)).astype(BF16)
                xs[2, frame, r, :, lanes] = jnp.where(
                    row_id == COLS - 1, right, pltpu.roll(n, COLS - 1, 0)
                ).astype(BF16)

        return step

    def normalize(stage, g):
        norm_edges(stage, g)

        def frame_step(f, carry):
            row_step = norm_rows(stage, 2 * g + f)

            def step(r, carry):
                row_step(r)
                return carry

            return lax.fori_loop(0, ROWS + 2, step, carry, unroll=9)

        lax.fori_loop(0, 2, frame_step, 0)

    def fold_weights():
        def step(u, carry):
            a = u // 8
            rows = pl.ds(pl.multiple_of(lax.rem(u, 8) * 32, 32), 32)
            k = [[w2[a * 9 + b * 3 + c, rows].astype(F32) for c in range(3)] for b in range(3)]
            upper = [k[1][c] + k[2][c] for c in range(3)]
            lower = [k[0][c] + k[1][c] for c in range(3)]
            for i, v in enumerate((k[0], upper, lower, k[2])):
                wc[a * 4 + i, rows, 0:CO] = (v[1] + v[2]).astype(BF16)
                wc[a * 4 + i, rows, CO : 2 * CO] = (v[0] + v[1]).astype(BF16)
            for q in range(2):
                we[a * 2 + q, rows, 0:CO] = upper[2 * q].astype(BF16)
                we[a * 2 + q, rows, CO : 2 * CO] = lower[2 * q].astype(BF16)
                wg[a * 2 + q, rows, 0:CO] = k[0][2 * q].astype(BF16)
                wg[a * 2 + q, rows, CO : 2 * CO] = k[2][2 * q].astype(BF16)
            return carry

        lax.fori_loop(0, 24, step, 0)

    def dot(x, w):
        return jnp.dot(x, w, preferred_element_type=F32)

    def flat(piece):
        return piece.reshape(-1, CH)

    def conv_one_row(b):
        total = acc1[...]
        for c in range(3):
            total = total + dot(flat(xs[c, 2:4, b : b + ROWS]), w1[18 + b * 3 + c])
        acc1[...] = total

    def conv_one(a):
        total = acc1[...]
        for b in range(3):
            for c in range(3):
                total = total + dot(flat(xs[c, pl.ds(a, 2), b : b + ROWS]), w1[a * 9 + b * 3 + c])
        acc1[...] = total

    def conv_two(a):
        for p in range(2):
            total = acc2[p]
            for d in range(2):
                total = total + dot(flat(xs[1, pl.ds(a, 2), p + d : p + d + ROWS]), wc[a * 4 + p * 2 + d])
            acc2[p] = total
        for q in range(2):
            acce[q] += dot(flat(xs[2 * q, pl.ds(a, 2), 1 : 1 + ROWS]), we[a * 2 + q])
            accg[q] += dot(flat(xs[2 * q, pl.ds(a, 2)]), wg[a * 2 + q])

    def beside(products, work):
        done = 0
        for i, product in enumerate(products):
            product()
            until = (i + 1) * len(work) // len(products)
            for n in range(done, until):
                work[n]()
            done = until

    def rows_before(stage):
        work = []
        for f in range(2):
            step = norm_rows(stage, f)
            work += [functools.partial(step, r) for r in range(ROWS + 2)]
        return work

    def products_two(a):
        def middle(p):
            total = acc2[p]
            for d in range(2):
                total = total + dot(flat(xs[1, a : a + 2, p + d : p + d + ROWS]), wc[a * 4 + p * 2 + d])
            acc2[p] = total

        def inner(q):
            acce[q] += dot(flat(xs[2 * q, a : a + 2, 1 : 1 + ROWS]), we[a * 2 + q])

        def outer(q):
            accg[q] += dot(flat(xs[2 * q, a : a + 2]), wg[a * 2 + q])

        return [functools.partial(f, i) for f in (middle, inner, outer) for i in range(2)]

    def chain_two():
        def middle(p, f, frames):
            place = slice(f * ROWS * COLS, (f + frames) * ROWS * COLS)
            total = acc2[p, place]
            for a in (1, 0):
                for d in range(2):
                    piece = xs[1, a + f : a + f + frames, p + d : p + d + ROWS]
                    total = total + dot(flat(piece), wc[a * 4 + p * 2 + d])
            acc2[p, place] = total

        def outputs(p, f):
            return [functools.partial(finish, p, f, i) for i in range(ROWS)]

        for q in range(2):
            total = acce[q]
            for a in (1, 0):
                total = total + dot(flat(xs[2 * q, a : a + 2, 1 : 1 + ROWS]), we[a * 2 + q])
            acce[q] = total
            total = accg[q]
            for a in (1, 0):
                total = total + dot(flat(xs[2 * q, a : a + 2]), wg[a * 2 + q])
            accg[q] = total
        middle(0, 0, 2)
        middle(1, 0, 1)
        for work in outputs(0, 0) + outputs(0, 1):
            work()
        middle(1, 1, 1)
        for f in range(2):
            for i, work in enumerate(outputs(1, f)):
                work()
                if i % 4 == 3:
                    store(f, i // 4).start()

    def store(f, part):
        rows = pl.ds(part * 8, 8)
        return pltpu.make_async_copy(ob.at[f, rows], out.at[f, rows], osem.at[f, part])

    def finish(p, f, i):
        slot = i % 8
        place = slice((f * ROWS + i) * COLS, (f * ROWS + i + 1) * COLS)
        row = f * (ROWS + 2) + i + 2 * p
        outer = slice(row * COLS, (row + 1) * COLS)
        for q in range(2):
            v = acc2[p, place, q * CO : (q + 1) * CO] + acce[q, place, p * CO : (p + 1) * CO]
            tmp[slot, pl.ds(q, COLS, stride=2), :] = v + accg[q, outer, p * CO : (p + 1) * CO]
        ob[f, i * 2 + p] = tmp[slot].astype(BF16)

    load_lat.wait()
    take_in(0, lambda f, r: buf[0, 2 + f, 1 + r].astype(F32))
    pl.semaphore_wait(ready, len(senders))
    start_plane(0)
    near, far = send_halo(0)
    for load in loads:
        load.wait()
    start_line(0)
    fold_weights()
    acc1[...] = jnp.zeros_like(acc1)
    end_line(0, prm[0], prm[1])
    for copy in near:
        copy.wait_recv()
    normalize(0, 1)
    for copy in far:
        copy.wait_recv()
    norm_edges(0, 0)
    beside([functools.partial(conv_one_row, b) for b in range(3)], rows_before(0))

    def tap_step(i, carry):
        conv_one(1 - i)
        return carry

    lax.fori_loop(0, 2, tap_step, 0)

    bias = jnp.concatenate([prm[2, 0:1], prm[2, 1:2]], axis=1)

    def block_out(f, r):
        conv = acc1[pl.ds(pl.multiple_of((f * ROWS + r) * COLS, COLS), COLS)]
        v = (buf[0, 2 + f, 1 + r].astype(F32) + conv + bias).astype(BF16)
        buf[1, 2 + f, 1 + r] = v
        return v.astype(F32)

    take_in(1, block_out)
    start_plane(1)
    near, far = send_halo(1)
    start_line(1)
    skip = dot(flat(buf[1, 2:4, 1 : ROWS + 1]), ws[...]) + b2[...]
    for p in range(2):
        for q in range(2):
            acc2[p, :, q * CO : (q + 1) * CO] = skip
    acce[...] = jnp.zeros_like(acce)
    accg[...] = jnp.zeros_like(accg)
    end_line(1, prm[3], prm[4])
    for copy in near:
        copy.wait_recv()
    normalize(1, 1)
    for copy in far:
        copy.wait_recv()
    norm_edges(1, 0)
    beside(products_two(2), rows_before(1))
    chain_two()

    for copy in sends:
        copy.wait_send()
    for stage in range(2):
        pltpu.make_async_copy(da.at[stage], da.at[stage], ssem_a.at[stage]).wait()
        pltpu.make_async_copy(db.at[stage], db.at[stage], ssem_b.at[stage]).wait()
    for f in range(2):
        for part in range(4):
            store(f, part).wait()


def on_device(
    latents, gain_one, shift_one, weight_one, bias_one, gain_two, shift_two, weight_two, weight_skip, bias_two
):
    vmem = pltpu.VMEM
    dma = pltpu.SemaphoreType.DMA
    n_halo = 2 * len(PIECES) + 2
    halves = lambda v: v.reshape(2, 128)
    return pl.pallas_call(
        kernel,
        out_shape=jax.ShapeDtypeStruct((2, 2 * ROWS, 2 * COLS, CO), BF16),
        in_specs=[pl.BlockSpec(memory_space=pl.ANY)] * 10,
        out_specs=pl.BlockSpec(memory_space=pl.ANY),
        scratch_shapes=[
            vmem((2, 4, ROWS + 2, COLS, CH), BF16),
            vmem((2, 2, 2 * ROWS, CH), BF16),
            vmem((2, 2, 2, 2 * ROWS, CH), BF16),
            vmem((2, 4, 2, CH), F32),
            vmem((2, 2, 4, 2, CH), F32),
            vmem((2, 2 * ROWS * COLS, 128), F32),
            vmem((3, 4, ROWS + 2, COLS, CH), BF16),
            vmem((2, 8 * 32, 128), F32),
            vmem((8, 128), F32),
            vmem((3, 8, 128), F32),
            vmem((2, 8, 128), F32),
            vmem((27, CH, CH), BF16),
            vmem((27, CH, CO), BF16),
            vmem((12, CH, 2 * CO), BF16),
            vmem((6, CH, 2 * CO), BF16),
            vmem((6, CH, 2 * CO), BF16),
            vmem((CH, CO), BF16),
            vmem((5, 2, 128), F32),
            vmem((1, CO), F32),
            vmem((2 * ROWS * COLS, CH), F32),
            vmem((2, 2 * ROWS * COLS, 2 * CO), F32),
            vmem((2, 2 * ROWS * COLS, 2 * CO), F32),
            vmem((2, 2 * (ROWS + 2) * COLS, 2 * CO), F32),
            vmem((8, 2 * COLS, CO), F32),
            vmem((2, 2 * ROWS, 2 * COLS, CO), BF16),
            vmem((2, 1, 128), F32),
            vmem((2, 1, 384), F32),
            vmem((2, len(PLANE), 1, 128), F32),
            vmem((2, len(LINE), 1, 384), F32),
            dma((2, n_halo)),
            dma((2, n_halo)),
            dma((2,)),
            dma((2,)),
            dma((2,)),
            dma((2,)),
            dma((10,)),
            dma((2, 4)),
        ],
        compiler_params=pltpu.CompilerParams(
            collective_id=0, has_side_effects=True, vmem_limit_bytes=62 << 20
        ),
    )(
        latents,
        weight_one.reshape(27, CH, CH),
        weight_two.reshape(27, CH, CO),
        weight_skip,
        halves(gain_one),
        halves(shift_one),
        halves(bias_one),
        halves(gain_two),
        halves(shift_two),
        bias_two.reshape(1, CO),
    )


def solution(mesh):
    in_specs = (P("ta", "gy", "gx", None),) + (P(),) * 9
    return jax.shard_map(
        on_device, mesh=mesh, in_specs=in_specs, out_specs=P("ta", "gy", "gx", None), check_vma=False
    )
```
